128 devices in a mesh: dp: 8 (over x, y_lo), tensor: 16 (over y_hi, z, core).
Axes of the slice: x: 4, y: 4 (y_hi: 2, y_lo: 2; y = y_hi * 2 + y_lo), z: 4, core: 2. Of those that a mesh axis runs over, the one named last changes fastest.
Arguments:
- gate_pre: bfloat16 [4096, 14848], P('dp', 'tensor'), may hold values from -6 to 6
- up_pre: bfloat16 [4096, 14848], P('dp', 'tensor'), may hold values from -6 to 6
- w_down: bfloat16 [14848, 8192], P('tensor', 'dp'), may hold values from -0.0625 to 0.0625
- cotangent: bfloat16 [4096, 8192], P('dp', 'tensor'), may hold values from -6 to 6
Outputs:
- layer_out: bfloat16 [4096, 8192], P('dp', 'tensor')
- grad_gate: bfloat16 [4096, 14848], P('dp', 'tensor')
- grad_up: bfloat16 [4096, 14848], P('dp', 'tensor')
- grad_down: bfloat16 [14848, 8192], P('tensor', 'dp')
The draws below stay inside these ranges and needn't reach their ends.
All inputs are finite; a program needn't handle non-finite values.
Results may differ from the reference program's by a relative error of at most 0.018.
Values may be sent and summed in bfloat16 or wider, within the bound.
A program may use at most 128 MiB of HBM per device.

```python
import jax
import jax.numpy as jnp
from jax import lax

D = 8192
FF = 14848
TOK_DEV = 512
TOKENS = 4096
N_DP = 8
N_TENSOR = 16


def spiked(result, own_key, source, target, shards_of, factor):
    owner, partner = [(jnp.arange(result.shape[position]) // (result.shape[position] // shards_of)).reshape([-1 if axis == position else 1 for axis in range(result.ndim)]) for position in (source, target)]
    chosen = jax.random.permutation(own_key, shards_of)[partner]
    strong = (owner == chosen) | (owner == (partner + shards_of // 2) % shards_of)
    return jnp.where(strong, factor * result, result)


def shard_levels(stream_key, dims, pieces, low, high):
    level, own = 1.0, jax.random.fold_in(stream_key, 6)
    for axis_at, parts in pieces:
        heights = jnp.exp(jax.random.uniform(jax.random.fold_in(own, axis_at), (parts,), jnp.float32, low / len(pieces), high / len(pieces)))
        level = level * jnp.repeat(heights, dims[axis_at] // parts).reshape([-1 if axis == axis_at else 1 for axis in range(len(dims))])
    return level


def normal_values(own_key, dims, scale, bound, pieces=(), dtype=jnp.bfloat16):
    array = jax.random.normal(own_key, dims, jnp.float32) * scale
    if len(pieces) > 0:
        array = shard_levels(own_key, dims, pieces, -0.22, 0.18) * array
    return jnp.clip(array, min=-bound, max=bound).astype(dtype)


def noise_with(rng, extent, scale, most, shards, heavy, held_as=jnp.bfloat16):
    array = scale * jax.random.normal(rng, extent, jnp.float32)
    if shards:
        array = array * shard_levels(rng, extent, shards, -0.22, 0.18)
    return jnp.clip(spiked(array, jax.random.fold_in(rng, 3), *heavy), -most, most).astype(held_as)


def setup_inputs(seed: int = 0) -> dict:
    splits = jax.random.split(jax.random.key(seed), 5)
    gate_pre = normal_values(splits[0], (TOKENS, FF), 1.0, 6.0, ((0, 8), (1, 16)))
    up_pre = normal_values(splits[1], (TOKENS, FF), 1.0, 6.0, ((0, 8), (1, 16)))
    w_down = noise_with(splits[2], (FF, D), FF ** -0.5, 0.0625, ((0, 16), (1, 8)), (0, 1, 16, 2.0))
    cotangent = noise_with(splits[3], (TOKENS, D), 1.0, 6.0, ((0, 8), (1, 16)), (0, 1, 16, 2.0))
    return dict(gate_pre=gate_pre, up_pre=up_pre, w_down=w_down, cotangent=cotangent)


def reference(gate_pre, up_pre, w_down, cotangent):
    gate_val = gate_pre.astype(jnp.float32)
    up_val = up_pre.astype(jnp.float32)
    squash = jax.nn.sigmoid(gate_val)
    hidden = (gate_val * squash * up_val).astype(jnp.bfloat16)
    width = FF // N_TENSOR
    summed = jnp.zeros((gate_pre.shape[0], D), jnp.float32)
    for block in range(N_TENSOR):
        partial_out = jnp.dot(hidden[:, block * width:(block + 1) * width], w_down[block * width:(block + 1) * width], preferred_element_type=jnp.float32)
        rounded = lax.optimization_barrier(partial_out.astype(jnp.bfloat16))
        summed = summed + rounded.astype(jnp.float32)
    layer_out = summed.astype(jnp.bfloat16)
    grad_hidden = jnp.dot(cotangent, w_down.T, preferred_element_type=jnp.float32)
    grad_up = (grad_hidden * gate_val * squash).astype(jnp.bfloat16)
    grad_gate = (grad_hidden * up_val * squash * (1.0 + gate_val * (1.0 - squash))).astype(jnp.bfloat16)
    weight_sum = jnp.zeros((FF, D), jnp.float32)
    for member in range(N_DP):
        rows_hidden = hidden[member * TOK_DEV:(member + 1) * TOK_DEV]
        rows_cot = cotangent[member * TOK_DEV:(member + 1) * TOK_DEV]
        term = jnp.dot(rows_hidden.T, rows_cot, preferred_element_type=jnp.float32)
        rounded = lax.optimization_barrier(term.astype(jnp.bfloat16))
        weight_sum = weight_sum + rounded.astype(jnp.float32)
    return layer_out, grad_gate, grad_up, weight_sum.astype(jnp.bfloat16)
```

```python
import jax
import jax.numpy as jnp
from jax import lax
from jax.experimental import pallas as pl
from jax.experimental.pallas import tpu as pltpu
from jax.sharding import PartitionSpec as P

MESH = pl.DeviceIdType.MESH
BF = jnp.bfloat16
F32 = jnp.float32

TOK = 512
FF = 928
DM = 1024
HALF = 512
CUT = 464
C = 2
RC = HALF // C
HC = RC // 2


class Copies:
    def __init__(self, send, recv):
        self.send, self.recv, self.all, self.n = send, recv, [], 0

    def put(self, src, dst, target, landing=None):
        k = self.n
        self.n += 1
        copy = pltpu.make_async_remote_copy(
            src, dst, self.send.at[k], self.recv.at[k], device_id=target, device_id_type=MESH
        )
        copy.start()
        self.all.append((None, copy))
        if landing is None:
            return copy
        return pltpu.make_async_remote_copy(
            src, landing, self.send.at[k], self.recv.at[k], device_id=target, device_id_type=MESH
        )

    def put_or_keep(self, keep, src, dst, target, landing):
        k = self.n
        self.n += 1
        copy = pltpu.make_async_remote_copy(
            src, dst, self.send.at[k], self.recv.at[k], device_id=target, device_id_type=MESH
        )
        own = pltpu.make_async_copy(src, dst, self.recv.at[k])
        pl.when(keep)(own.start)
        pl.when(jnp.logical_not(keep))(copy.start)
        self.all.append((keep, copy))
        got = pltpu.make_async_remote_copy(
            src, landing, self.send.at[k], self.recv.at[k], device_id=target, device_id_type=MESH
        )

        def wait():
            pl.when(keep)(own.wait)
            pl.when(jnp.logical_not(keep))(got.wait_recv)

        return wait

    def finish(self):
        for keep, copy in self.all:
            if keep is None:
                copy.wait_send()
            else:
                pl.when(jnp.logical_not(keep))(copy.wait_send)


def nn(a, b):
    return lax.dot_general(a, b, (((1,), (0,)), ((), ())), preferred_element_type=F32)


def nt(a, b):
    return lax.dot_general(a, b, (((1,), (1,)), ((), ())), preferred_element_type=F32)


def kernel(
    gate, up, w, cot, lay_out, gg_out, gu_out, gd_out,
    HT, CT, WT, OWN, ZM, G, R1, R3, RAB, RO, LO, LS, LX, LH, LD, LY, FIN, SWP,
    acc, gd_stage, lay_stage, gg_stage, gu_stage, send_sem, recv_sem, out_sem,
):
    dp, t = lax.axis_index("dp"), lax.axis_index("tensor")
    x, yl = dp // 2, dp % 2
    yh, z, c = t // 8, (t // 2) % 4, t % 2
    j = t // 2

    def X(d):
        return (((x + d + 4) % 4) * 2 + yl, t)

    def Z(d):
        return (dp, yh * 8 + ((z + d + 4) % 4) * 2 + c)

    YL = (x * 2 + 1 - yl, t)
    YH = (dp, (1 - yh) * 8 + z * 2 + c)
    CORE = (dp, t + 1 - 2 * c)
    T1, T1S = Z(x), Z(4 - x)
    zs = (z - x + 4) % 4
    T2 = ((2 * yh + zs // 2) * 2 + zs % 2, ((yl + yh + zs) % 2) * 8 + z * 2 + c)
    zo = 2 * (x % 2) + yl
    xs, yls = (z - zo + 4) % 4, (yh + x // 2 + yl) % 2
    T2S = (xs * 2 + yls, (x // 2) * 8 + z * 2 + c)
    q = xs * 2 + yls
    SW = (q, 2 * dp + c)
    xi, yli = j // 2, j % 2
    zi = 2 * (xi % 2) + yli
    SWS = (j, ((yl + xi // 2 + yli) % 2) * 8 + ((x + zi) % 4) * 2 + c)
    t1_keep = x == 0
    t2_keep = jnp.logical_and(T2[0] == dp, T2[1] == t)
    sw_keep = jnp.logical_and(SW[0] == dp, SW[1] == t)

    def tok(dx, other):
        row = 1 - yl if other else yl
        return ((x + dx + 4) % 4) * 2 + row

    def slot(g):
        return ((g % 2 + x // 2 + yl) % 2) * 4 + (g // 2 + zo) % 4

    def place(dz, other):
        row = 1 - yh if other else yh
        return row * 4 + (z + dz + 4) % 4

    barrier = pltpu.get_barrier_semaphore()
    greeted = (X(1), X(-1), YL, Z(1), Z(-1), YH, CORE, T1, T1S, T2, T2S, SW, SWS)
    for other in greeted:
        pl.semaphore_signal(barrier, inc=1, device_id=other, device_id_type=MESH)

    for r in range(0, HALF, 128):
        OWN[:, r : r + 128] = cot[r : r + 128, :].astype(F32).T.astype(BF)

    def make_hidden(k, _):
        rows = pl.ds(pl.multiple_of(k * 128, 128), 128)
        g = gate[rows, :].astype(F32)
        h = g * jax.nn.sigmoid(g) * up[rows, :].astype(F32)
        HT[dp, :, rows] = h.T.astype(BF)
        return 0

    lax.fori_loop(0, 4, make_hidden, 0)

    pl.semaphore_wait(barrier, len(greeted))
    cp = Copies(send_sem, recv_sem)

    def piece(ref, *at, k):
        return ref.at[(*at, pl.ds(k * RC, RC))]

    def crow(k, size=RC):
        return pl.ds(pl.multiple_of(c * HALF + k, 16), size)

    t1 = [cp.put_or_keep(t1_keep, OWN.at[pl.ds(k * RC, RC)], ZM.at[pl.ds(k * RC, RC)], T1, ZM.at[pl.ds(k * RC, RC)]) for k in range(C)]
    own = HT.at[dp]
    s1y = cp.put(own, own, YL, HT.at[tok(0, True)])
    s1p = cp.put(own, own, X(1), HT.at[tok(-1, False)])
    s1m = cp.put(own, own, X(-1), HT.at[tok(1, False)])

    for r in range(0, FF, 464):
        WT[:, r : r + 464] = w[r : r + 464, :].astype(F32).T.astype(BF)

    t2_place = (T2[1] // 2)
    t2 = []
    for k in range(C):
        t1[k]()
        t2.append(cp.put_or_keep(t2_keep, ZM.at[pl.ds(k * RC, RC)], CT.at[t2_place, crow(k * RC)], T2, CT.at[j, crow(k * RC)]))

    def make_layer(g):
        s = slot(g)

        def part(k, _):
            cols = pl.ds(pl.multiple_of(k * 256, 256), 256)
            here = pl.ds(pl.multiple_of(c * HALF, HALF), HALF)
            there = pl.ds(pl.multiple_of((1 - c) * HALF, HALF), HALF)
            h = HT[g, :, cols]
            LS[s, :, cols] = nn(WT[there, :], h).astype(BF)
            LO[s, :, cols] = nn(WT[here, :], h).astype(BF)
            return 0

        lax.fori_loop(0, 2, part, 0)
        return cp.put(LS.at[s], LX.at[s], CORE)

    lx = [make_layer(dp)]

    def spread(block, k):
        ref = CT.at[block, crow(k * RC)]
        return cp.put(ref, ref, Z(1)), cp.put(ref, ref, Z(-1))

    def forward(row, k):
        a = CT.at[place(-1, row), crow(k * RC, HC)]
        b = CT.at[place(1, row), crow(k * RC + HC, HC)]
        return cp.put(a, a, Z(1)), cp.put(b, b, Z(-1))

    t3, near_own, near_par = [], [], []
    for k in range(C):
        t2[k]()
        ref = CT.at[j, crow(k * RC)]
        t3.append(cp.put(ref, ref, YH))
        near_own.append(spread(j, k))
    t5 = []

    def cross(block):
        ref = CT.at[block, crow(0, HALF)]
        t5.append(cp.put(ref, ref, CORE))

    cross(j)

    s1p.wait_recv()
    a = HT.at[tok(-1, False), pl.ds(0, CUT)]
    s2a = cp.put(a, a, X(1))
    s1m.wait_recv()
    b = HT.at[tok(1, False), pl.ds(CUT, FF - CUT)]
    s2b = cp.put(b, b, X(-1))
    s1y.wait_recv()
    par = HT.at[tok(0, True)]
    s3p = cp.put(par, par, X(1))
    s3m = cp.put(par, par, X(-1))

    for k in range(C):
        t3[k].wait_recv()
        near_par.append(spread(place(0, True), k))
    cross(place(0, True))

    lx.append(make_layer(tok(0, True)))
    lx.append(make_layer(tok(1, False)))
    lx.append(make_layer(tok(-1, False)))

    far = []
    for row, near in ((False, near_own), (True, near_par)):
        for k in range(C):
            near[k][0].wait_recv()
            near[k][1].wait_recv()
            far.extend(forward(row, k))
        cross(place(1, row))
        cross(place(-1, row))

    s2a.wait_recv()
    s2b.wait_recv()
    two = HT.at[tok(2, False)]
    s4 = cp.put(two, two, YL)
    lx.append(make_layer(tok(2, False)))

    for f in far[: 2 * C]:
        f.wait_recv()
    cross(place(2, False))
    for f in far[2 * C :]:
        f.wait_recv()
    cross(place(2, True))
    s3p.wait_recv()
    s3m.wait_recv()
    lx.append(make_layer(tok(1, True)))
    lx.append(make_layer(tok(-1, True)))
    for f in t5:
        f.wait_recv()

    def make_grad(g):
        s = slot(g)

        def part(k, _):
            cols = pl.ds(pl.multiple_of(k * 256, 256), 256)
            G[g, :, cols] = nn(w[...], CT[s, :, cols]).astype(BF)
            return 0

        lax.fori_loop(0, 2, part, 0)

    make_grad(tok(1, True))
    g3p = cp.put(G.at[tok(1, True)], R3.at[0], X(1))
    make_grad(tok(-1, True))
    g3m = cp.put(G.at[tok(-1, True)], R3.at[1], X(-1))
    make_grad(tok(2, True))
    g1 = cp.put(G.at[tok(2, True)], R1, YL)
    s4.wait_recv()
    lx.append(make_layer(tok(2, True)))

    for f in lx:
        f.wait_recv()

    def pair(block):
        LO[block] = (LO[block].astype(F32) + LX[block].astype(F32)).astype(BF)

    halves, directs = {}, {}
    for n, row in enumerate((True, False)):
        two = place(2, row)
        pair(two)
        for k in range(C):
            halves[n, k] = (
                cp.put(LO.at[two, pl.ds(k * RC, HC)], LH.at[n, 0, k], Z(1)),
                cp.put(LO.at[two, pl.ds(k * RC + HC, HC)], LH.at[n, 1, k], Z(-1)),
            )
        pair(place(1, row))
        pair(place(-1, row))
    for dx in (2, 1, -1):
        make_grad(tok(dx, False))
    for n, row in enumerate((True, False)):
        for k in range(C):
            sent = []
            for side, dz in ((0, 1), (1, -1)):
                block = place(dz, row)
                halves[n, k][side].wait_recv()
                at = pl.ds(k * RC + side * HC, HC)
                LO[block, at] = (LO[block, at].astype(F32) + LH[n, side, k].astype(F32)).astype(BF)
                at = pl.ds(k * RC, RC)
                sent.append(cp.put(LO.at[block, at], LD.at[n, side, at], Z(dz)))
            directs[n, k] = sent
    pair(place(0, True))
    make_grad(tok(0, True))

    g1.wait_recv()
    two = tok(2, False)
    G[two] = (G[two].astype(F32) + R1[...].astype(F32)).astype(BF)
    g2a = cp.put(G.at[two, pl.ds(0, CUT)], RAB.at[pl.ds(0, CUT)], X(1))
    g2b = cp.put(G.at[two, pl.ds(CUT, FF - CUT)], RAB.at[pl.ds(CUT, FF - CUT)], X(-1))
    make_grad(dp)

    def weight_grad(n):
        cols = pl.ds(n * 256, 256)
        acc[...] = jnp.zeros_like(acc)

        def add(g, _):
            acc[...] += nt(HT[g], CT[slot(g), cols, :])
            return 0

        lax.fori_loop(0, 8, add, 0)
        gd_stage[n % 2] = acc[...].astype(BF)
        copy = pltpu.make_async_copy(gd_stage.at[n % 2], gd_out.at[:, cols], out_sem.at[n])
        copy.start()
        return copy

    outs = [weight_grad(0)]

    g3p.wait_recv()
    g3m.wait_recv()
    par = tok(0, True)
    G[par] = (G[par].astype(F32) + R3[0].astype(F32) + R3[1].astype(F32)).astype(BF)
    g4 = cp.put(G.at[par], RO.at[2], YL)

    ly = []
    block = place(0, True)
    for k in range(C):
        at = pl.ds(k * RC, RC)
        directs[0, k][0].wait_recv()
        directs[0, k][1].wait_recv()
        LO[block, at] = (
            LO[block, at].astype(F32) + LD[0, 0, at].astype(F32) + LD[0, 1, at].astype(F32)
        ).astype(BF)
        ly.append(cp.put(LO.at[block, at], LY.at[at], YH))

    g2a.wait_recv()
    g2b.wait_recv()
    for side, dx, at in ((0, 1, pl.ds(0, CUT)), (1, -1, pl.ds(CUT, FF - CUT))):
        block = tok(dx, False)
        G[block, at] = (G[block, at].astype(F32) + RAB[at].astype(F32)).astype(BF)
        sent = cp.put(G.at[block], RO.at[side], X(dx))
        if side == 0:
            g5p = sent
        else:
            g5m = sent

    outs.append(weight_grad(1))

    block = j
    pair(block)
    sw = []
    for k in range(C):
        at = pl.ds(k * RC, RC)
        directs[1, k][0].wait_recv()
        directs[1, k][1].wait_recv()
        ly[k].wait_recv()
        FIN[at] = (
            LO[block, at].astype(F32) + LD[1, 0, at].astype(F32) + LD[1, 1, at].astype(F32) + LY[at].astype(F32)
        ).astype(BF)
        sw.append(cp.put_or_keep(sw_keep, FIN.at[at], SWP.at[at], SW, SWP.at[at]))
    outs[0].wait()
    outs.append(weight_grad(2))
    outs[1].wait()
    outs.append(weight_grad(3))

    for k in range(C):
        sw[k]()
        at = pl.ds(k * RC, RC)
        for r in range(0, TOK, 128):
            lay_stage[r : r + 128, k * RC : (k + 1) * RC] = SWP[at, r : r + 128].astype(F32).T.astype(BF)
    copy = pltpu.make_async_copy(lay_stage, lay_out, out_sem.at[4])
    copy.start()
    outs.append(copy)

    g4.wait_recv()
    g5p.wait_recv()
    g5m.wait_recv()

    def finish(k, _):
        rows = pl.ds(pl.multiple_of(k * 128, 128), 128)
        total = G[dp, :, rows].astype(F32)
        for side in range(3):
            total = total + RO[side, :, rows].astype(F32)
        total = total.T
        g = gate[rows, :].astype(F32)
        squash = jax.nn.sigmoid(g)
        gu_stage[rows, :] = (total * g * squash).astype(BF)
        gg_stage[rows, :] = (
            total * up[rows, :].astype(F32) * squash * (1.0 + g * (1.0 - squash))
        ).astype(BF)
        return 0

    lax.fori_loop(0, 4, finish, 0)
    for n, (stage, out) in enumerate(((gg_stage, gg_out), (gu_stage, gu_out))):
        copy = pltpu.make_async_copy(stage, out, out_sem.at[5 + n])
        copy.start()
        outs.append(copy)
    cp.finish()
    for copy in outs[2:]:
        copy.wait()


def shards(gate_pre, up_pre, w_down, cotangent):
    vmem = pl.BlockSpec(memory_space=pltpu.VMEM)
    anywhere = pl.BlockSpec(memory_space=pl.ANY)
    n_copies = 100
    flops = 2 * 3 * TOK * FF * 8192
    return pl.pallas_call(
        kernel,
        out_shape=(
            jax.ShapeDtypeStruct((TOK, HALF), BF),
            jax.ShapeDtypeStruct((TOK, FF), BF),
            jax.ShapeDtypeStruct((TOK, FF), BF),
            jax.ShapeDtypeStruct((FF, DM), BF),
        ),
        in_specs=[vmem] * 4,
        out_specs=[anywhere] * 4,
        scratch_shapes=[
            pltpu.VMEM((8, FF, TOK), BF),
            pltpu.VMEM((8, DM, TOK), BF),
            pltpu.VMEM((DM, FF), BF),
            pltpu.VMEM((HALF, TOK), BF),
            pltpu.VMEM((HALF, TOK), BF),
            pltpu.VMEM((8, FF, TOK), BF),
            pltpu.VMEM((FF, TOK), BF),
            pltpu.VMEM((2, FF, TOK), BF),
            pltpu.VMEM((FF, TOK), BF),
            pltpu.VMEM((3, FF, TOK), BF),
            pltpu.VMEM((8, HALF, TOK), BF),
            pltpu.VMEM((8, HALF, TOK), BF),
            pltpu.VMEM((8, HALF, TOK), BF),
            pltpu.VMEM((2, 2, C, HC, TOK), BF),
            pltpu.VMEM((2, 2, HALF, TOK), BF),
            pltpu.VMEM((HALF, TOK), BF),
            pltpu.VMEM((HALF, TOK), BF),
            pltpu.VMEM((HALF, TOK), BF),
            pltpu.VMEM((FF, 256), F32),
            pltpu.VMEM((2, FF, 256), BF),
            pltpu.VMEM((TOK, HALF), BF),
            pltpu.VMEM((TOK, FF), BF),
            pltpu.VMEM((TOK, FF), BF),
            pltpu.SemaphoreType.DMA((n_copies,)),
            pltpu.SemaphoreType.DMA((n_copies,)),
            pltpu.SemaphoreType.DMA((7,)),
        ],
        compiler_params=pltpu.CompilerParams(
            collective_id=0, has_side_effects=True, vmem_limit_bytes=64 * 2**20
        ),
        cost_estimate=pl.CostEstimate(flops=flops, bytes_accessed=2**24, transcendentals=0),
    )(gate_pre, up_pre, w_down, cotangent)


def solution(mesh):
    placed = (P("dp", "tensor"), P("dp", "tensor"), P("tensor", "dp"), P("dp", "tensor"))
    return jax.shard_map(
        shards,
        mesh=mesh,
        in_specs=placed,
        out_specs=(P("dp", "tensor"), P("dp", "tensor"), P("dp", "tensor"), P("tensor", "dp")),
        check_vma=False,
    )
```

```python
import jax
import jax.numpy as jnp
from jax import lax
from jax.experimental import pallas as pl
from jax.experimental.pallas import tpu as pltpu
from jax.sharding import PartitionSpec as P

MESH = pl.DeviceIdType.MESH
BF = jnp.bfloat16
F32 = jnp.float32

TOK = 512
FF = 928
DM = 1024
HALF = 512
CUT = 464
C = 2
RC = HALF // C
HC = RC // 2


class Copies:
    def __init__(self, send, recv):
        self.send, self.recv, self.all, self.n = send, recv, [], 0

    def put(self, src, dst, target, landing=None):
        k = self.n
        self.n += 1
        copy = pltpu.make_async_remote_copy(
            src, dst, self.send.at[k], self.recv.at[k], device_id=target, device_id_type=MESH
        )
        copy.start()
        self.all.append((None, copy))
        if landing is None:
            return copy
        return pltpu.make_async_remote_copy(
            src, landing, self.send.at[k], self.recv.at[k], device_id=target, device_id_type=MESH
        )

    def put_or_keep(self, keep, src, dst, target, landing):
        k = self.n
        self.n += 1
        copy = pltpu.make_async_remote_copy(
            src, dst, self.send.at[k], self.recv.at[k], device_id=target, device_id_type=MESH
        )
        own = pltpu.make_async_copy(src, dst, self.recv.at[k])
        pl.when(keep)(own.start)
        pl.when(jnp.logical_not(keep))(copy.start)
        self.all.append((keep, copy))
        got = pltpu.make_async_remote_copy(
            src, landing, self.send.at[k], self.recv.at[k], device_id=target, device_id_type=MESH
        )

        def wait():
            pl.when(keep)(own.wait)
            pl.when(jnp.logical_not(keep))(got.wait_recv)

        return wait

    def finish(self):
        for keep, copy in self.all:
            if keep is None:
                copy.wait_send()
            else:
                pl.when(jnp.logical_not(keep))(copy.wait_send)


def nn(a, b):
    return lax.dot_general(a, b, (((1,), (0,)), ((), ())), preferred_element_type=F32)


def nt(a, b):
    return lax.dot_general(a, b, (((1,), (1,)), ((), ())), preferred_element_type=F32)


def kernel(
    gate_in, up_in, w_in, cot_in, lay_out, gg_out, gu_out, gd_out,
    gate, up, w, cot, HT, CT, WT, OWN, ZM, G, R1, R3, RAB, RO, LO, LS, LX, LH, LD, LY, FIN, SWP,
    acc, gd_stage, lay_stage, gg_stage, gu_stage, send_sem, recv_sem, in_sem, out_sem,
):
    dp, t = lax.axis_index("dp"), lax.axis_index("tensor")
    x, yl = dp // 2, dp % 2
    yh, z, c = t // 8, (t // 2) % 4, t % 2
    j = t // 2

    def X(d):
        return (((x + d + 4) % 4) * 2 + yl, t)

    def Z(d):
        return (dp, yh * 8 + ((z + d + 4) % 4) * 2 + c)

    YL = (x * 2 + 1 - yl, t)
    YH = (dp, (1 - yh) * 8 + z * 2 + c)
    CORE = (dp, t + 1 - 2 * c)
    T1, T1S = Z(x), Z(4 - x)
    zs = (z - x + 4) % 4
    T2 = ((2 * yh + zs // 2) * 2 + zs % 2, ((yl + yh + zs) % 2) * 8 + z * 2 + c)
    zo = 2 * (x % 2) + yl
    xs, yls = (z - zo + 4) % 4, (yh + x // 2 + yl) % 2
    T2S = (xs * 2 + yls, (x // 2) * 8 + z * 2 + c)
    q = xs * 2 + yls
    SW = (q, 2 * dp + c)
    xi, yli = j // 2, j % 2
    zi = 2 * (xi % 2) + yli
    SWS = (j, ((yl + xi // 2 + yli) % 2) * 8 + ((x + zi) % 4) * 2 + c)
    t1_keep = x == 0
    t2_keep = jnp.logical_and(T2[0] == dp, T2[1] == t)
    sw_keep = jnp.logical_and(SW[0] == dp, SW[1] == t)

    def tok(dx, other):
        row = 1 - yl if other else yl
        return ((x + dx + 4) % 4) * 2 + row

    def slot(g):
        return ((g % 2 + x // 2 + yl) % 2) * 4 + (g // 2 + zo) % 4

    def place(dz, other):
        row = 1 - yh if other else yh
        return row * 4 + (z + dz + 4) % 4

    barrier = pltpu.get_barrier_semaphore()
    greeted = (X(1), X(-1), YL, Z(1), Z(-1), YH, CORE, T1, T1S, T2, T2S, SW, SWS)
    for other in greeted:
        pl.semaphore_signal(barrier, inc=1, device_id=other, device_id_type=MESH)
    loads = []
    for n, (src, dst) in enumerate(((cot_in, cot), (gate_in, gate), (up_in, up), (w_in, w))):
        loads.append(pltpu.make_async_copy(src, dst, in_sem.at[n]))
        loads[-1].start()

    loads[0].wait()
    for r in range(0, HALF, 128):
        OWN[:, r : r + 128] = cot[r : r + 128, :].astype(F32).T.astype(BF)
    loads[1].wait()
    loads[2].wait()

    def make_hidden(k, _):
        rows = pl.ds(pl.multiple_of(k * 32, 32), 32)
        g = gate[rows, :].astype(F32)
        HT[dp, rows, :] = (g * jax.nn.sigmoid(g) * up[rows, :].astype(F32)).astype(BF)
        return 0

    pl.semaphore_wait(barrier, len(greeted))
    cp = Copies(send_sem, recv_sem)
    low, high = pl.ds(0, CUT), pl.ds(CUT, FF - CUT)

    def crow(k, size=RC):
        return pl.ds(pl.multiple_of(c * HALF + k, 16), size)

    def share(ref, target):
        return cp.put(ref, ref, target)

    t1, t2 = [], []
    for k in range(C):
        at = pl.ds(k * RC, RC)
        t1.append(cp.put_or_keep(t1_keep, OWN.at[at], ZM.at[at], T1, ZM.at[at]))
    lax.fori_loop(0, 29, make_hidden, 0)
    s1p, s1m = [share(HT.at[dp, low], X(1))], [share(HT.at[dp, high], X(-1))]
    s1y = share(HT.at[dp], YL)

    loads[3].wait()
    for r in range(0, FF, CUT):
        WT[:, r : r + CUT] = w[r : r + CUT, :].astype(F32).T.astype(BF)

    t2_place = T2[1] // 2
    for k in range(C):
        t1[k]()
        t2.append(cp.put_or_keep(t2_keep, ZM.at[pl.ds(k * RC, RC)], CT.at[t2_place, crow(k * RC)], T2, CT.at[j, crow(k * RC)]))

    def make_layer(g):
        s = slot(g)

        def part(k, _):
            cols = pl.ds(pl.multiple_of(k * 256, 256), 256)
            here = pl.ds(pl.multiple_of(c * HALF, HALF), HALF)
            there = pl.ds(pl.multiple_of((1 - c) * HALF, HALF), HALF)
            h = HT[g, :, cols]
            LS[s, :, cols] = nn(WT[there, :], h).astype(BF)
            LO[s, :, cols] = nn(WT[here, :], h).astype(BF)
            return 0

        lax.fori_loop(0, 2, part, 0)
        return cp.put(LS.at[s], LX.at[s], CORE)

    lx = [make_layer(dp)]

    s1p[0].wait_recv()
    s1m[0].wait_recv()
    s2 = [share(HT.at[tok(-1, False), low], X(1)), share(HT.at[tok(1, False), high], X(-1))]
    s1p.append(share(HT.at[dp, high], X(1)))
    s1m.append(share(HT.at[dp, low], X(-1)))

    def spread(block, k):
        ref = CT.at[block, crow(k * RC)]
        return share(ref, Z(1)), share(ref, Z(-1))

    def forward(row, k):
        a = CT.at[place(-1, row), crow(k * RC, HC)]
        b = CT.at[place(1, row), crow(k * RC + HC, HC)]
        return share(a, Z(1)), share(b, Z(-1))

    t3, t5, near = [], [], {}

    def cross(block):
        t5.append(share(CT.at[block, crow(0, HALF)], CORE))

    for k in range(C):
        t2[k]()
        t3.append(share(CT.at[j, crow(k * RC)], YH))
        near[False, k] = spread(j, k)
    cross(j)
    s1y.wait_recv()
    par = HT.at[tok(0, True)]
    s3p, s3m = share(par, X(1)), share(par, X(-1))

    for k in range(C):
        t3[k].wait_recv()
        near[True, k] = spread(place(0, True), k)
    s2[0].wait_recv()
    s2[1].wait_recv()
    s4 = share(HT.at[tok(2, False)], YL)
    cross(place(0, True))
    lx.append(make_layer(tok(0, True)))
    lx.append(make_layer(tok(2, False)))

    far = {}
    for row in (False, True):
        for k in range(C):
            near[row, k][0].wait_recv()
            near[row, k][1].wait_recv()
            far[row, k] = forward(row, k)
        cross(place(1, row))
        cross(place(-1, row))
    s1p[1].wait_recv()
    s1m[1].wait_recv()
    lx.append(make_layer(tok(1, False)))
    lx.append(make_layer(tok(-1, False)))
    for row in (False, True):
        for k in range(C):
            far[row, k][0].wait_recv()
            far[row, k][1].wait_recv()
        cross(place(2, row))
    for f in t5:
        f.wait_recv()

    def make_grad(g):
        s = slot(g)

        def part(k, _):
            cols = pl.ds(pl.multiple_of(k * 256, 256), 256)
            G[g, :, cols] = nn(w[...], CT[s, :, cols]).astype(BF)
            return 0

        lax.fori_loop(0, 2, part, 0)

    make_grad(tok(2, True))
    g1 = cp.put(G.at[tok(2, True)], R1, YL)
    make_grad(tok(1, True))
    g3p = cp.put(G.at[tok(1, True)], R3.at[0], X(1))
    make_grad(tok(-1, True))
    g3m = cp.put(G.at[tok(-1, True)], R3.at[1], X(-1))
    for g in (tok(2, False), tok(1, False), tok(-1, False), tok(0, True), dp):
        make_grad(g)

    s4.wait_recv()
    lx.append(make_layer(tok(2, True)))
    s3p.wait_recv()
    lx.append(make_layer(tok(-1, True)))
    s3m.wait_recv()
    lx.append(make_layer(tok(1, True)))
    for f in lx:
        f.wait_recv()

    def pair(block):
        LO[block] = (LO[block].astype(F32) + LX[block].astype(F32)).astype(BF)

    halves, directs = {}, {}
    for n, row in enumerate((True, False)):
        two = place(2, row)
        pair(two)
        for k in range(C):
            halves[n, k] = (
                cp.put(LO.at[two, pl.ds(k * RC, HC)], LH.at[n, 0, k], Z(1)),
                cp.put(LO.at[two, pl.ds(k * RC + HC, HC)], LH.at[n, 1, k], Z(-1)),
            )
    for row in (True, False):
        pair(place(1, row))
        pair(place(-1, row))

    def relay(n, row, k):
        sent = []
        for side, dz in ((0, 1), (1, -1)):
            block = place(dz, row)
            halves[n, k][side].wait_recv()
            at = pl.ds(k * RC + side * HC, HC)
            LO[block, at] = (LO[block, at].astype(F32) + LH[n, side, k].astype(F32)).astype(BF)
            at = pl.ds(k * RC, RC)
            sent.append(cp.put(LO.at[block, at], LD.at[n, side, at], Z(dz)))
        directs[n, k] = sent

    for n, row in enumerate((True, False)):
        for k in range(C):
            relay(n, row, k)
    pair(place(0, True))
    pair(j)

    def weight_grad(n):
        cols = pl.ds(n * 256, 256)
        acc[...] = jnp.zeros_like(acc)

        def add(g, _):
            acc[...] += nt(HT[g], CT[slot(g), cols, :])
            return 0

        lax.fori_loop(0, 8, add, 0)
        gd_stage[n % 2] = acc[...].astype(BF)
        copy = pltpu.make_async_copy(gd_stage.at[n % 2], gd_out.at[:, cols], out_sem.at[n])
        copy.start()
        return copy

    outs = [weight_grad(0)]
    g1.wait_recv()
    two = tok(2, False)
    G[two] = (G[two].astype(F32) + R1[...].astype(F32)).astype(BF)
    g2a = cp.put(G.at[two, low], RAB.at[low], X(1))
    g2b = cp.put(G.at[two, high], RAB.at[high], X(-1))
    up_one, down_one = tok(1, False), tok(-1, False)
    g5 = [cp.put(G.at[up_one, high], RO.at[0, high], X(1)), cp.put(G.at[down_one, low], RO.at[1, low], X(-1))]

    ly = []
    block = place(0, True)
    for k in range(C):
        at = pl.ds(k * RC, RC)
        directs[0, k][0].wait_recv()
        directs[0, k][1].wait_recv()
        LO[block, at] = (
            LO[block, at].astype(F32) + LD[0, 0, at].astype(F32) + LD[0, 1, at].astype(F32)
        ).astype(BF)
        ly.append(cp.put(LO.at[block, at], LY.at[at], YH))
    g3p.wait_recv()
    g3m.wait_recv()
    par = tok(0, True)
    G[par] = (G[par].astype(F32) + R3[0].astype(F32) + R3[1].astype(F32)).astype(BF)
    g5.append(cp.put(G.at[par], RO.at[2], YL))

    outs.append(weight_grad(1))

    sw = []
    for k in range(C):
        at = pl.ds(k * RC, RC)
        directs[1, k][0].wait_recv()
        directs[1, k][1].wait_recv()
        ly[k].wait_recv()
        FIN[at] = (
            LO[j, at].astype(F32) + LD[1, 0, at].astype(F32) + LD[1, 1, at].astype(F32) + LY[at].astype(F32)
        ).astype(BF)
        sw.append(cp.put_or_keep(sw_keep, FIN.at[at], SWP.at[at], SW, SWP.at[at]))

    g2a.wait_recv()
    G[up_one, low] = (G[up_one, low].astype(F32) + RAB[low].astype(F32)).astype(BF)
    g5.append(cp.put(G.at[up_one, low], RO.at[0, low], X(1)))
    g2b.wait_recv()
    G[down_one, high] = (G[down_one, high].astype(F32) + RAB[high].astype(F32)).astype(BF)
    g5.append(cp.put(G.at[down_one, high], RO.at[1, high], X(-1)))

    outs[0].wait()
    outs.append(weight_grad(2))
    outs[1].wait()
    outs.append(weight_grad(3))

    for k in range(C):
        sw[k]()
        at = pl.ds(k * RC, RC)
        for r in range(0, TOK, 128):
            lay_stage[r : r + 128, k * RC : (k + 1) * RC] = SWP[at, r : r + 128].astype(F32).T.astype(BF)
    copy = pltpu.make_async_copy(lay_stage, lay_out, out_sem.at[4])
    copy.start()
    outs.append(copy)

    for f in g5:
        f.wait_recv()

    def finish(k, _):
        rows = pl.ds(pl.multiple_of(k * 32, 32), 32)
        total = G[dp, rows, :].astype(F32)
        for side in range(3):
            total = total + RO[side, rows, :].astype(F32)
        g = gate[rows, :].astype(F32)
        squash = jax.nn.sigmoid(g)
        gu_stage[rows, :] = (total * g * squash).astype(BF)
        gg_stage[rows, :] = (
            total * up[rows, :].astype(F32) * squash * (1.0 + g * (1.0 - squash))
        ).astype(BF)
        return 0

    lax.fori_loop(0, 29, finish, 0)
    for n, (stage, out) in enumerate(((gg_stage, gg_out), (gu_stage, gu_out))):
        copy = pltpu.make_async_copy(stage, out, out_sem.at[5 + n])
        copy.start()
        outs.append(copy)
    cp.finish()
    for copy in outs[2:]:
        copy.wait()


def shards(gate_pre, up_pre, w_down, cotangent):
    anywhere = pl.BlockSpec(memory_space=pl.ANY)
    n_copies = 100
    flops = 2 * 3 * TOK * FF * 8192
    layer_out, grad_gate, grad_up, grad_down = pl.pallas_call(
        kernel,
        out_shape=(
            jax.ShapeDtypeStruct((TOK, HALF), BF),
            jax.ShapeDtypeStruct((FF, TOK), BF),
            jax.ShapeDtypeStruct((FF, TOK), BF),
            jax.ShapeDtypeStruct((FF, DM), BF),
        ),
        in_specs=[anywhere] * 4,
        out_specs=[anywhere] * 4,
        scratch_shapes=[
            pltpu.VMEM((FF, TOK), BF),
            pltpu.VMEM((FF, TOK), BF),
            pltpu.VMEM((FF, DM), BF),
            pltpu.VMEM((TOK, HALF), BF),
            pltpu.VMEM((8, FF, TOK), BF),
            pltpu.VMEM((8, DM, TOK), BF),
            pltpu.VMEM((DM, FF), BF),
            pltpu.VMEM((HALF, TOK), BF),
            pltpu.VMEM((HALF, TOK), BF),
            pltpu.VMEM((8, FF, TOK), BF),
            pltpu.VMEM((FF, TOK), BF),
            pltpu.VMEM((2, FF, TOK), BF),
            pltpu.VMEM((FF, TOK), BF),
            pltpu.VMEM((3, FF, TOK), BF),
            pltpu.VMEM((8, HALF, TOK), BF),
            pltpu.VMEM((8, HALF, TOK), BF),
            pltpu.VMEM((8, HALF, TOK), BF),
            pltpu.VMEM((2, 2, C, HC, TOK), BF),
            pltpu.VMEM((2, 2, HALF, TOK), BF),
            pltpu.VMEM((HALF, TOK), BF),
            pltpu.VMEM((HALF, TOK), BF),
            pltpu.VMEM((HALF, TOK), BF),
            pltpu.VMEM((FF, 256), F32),
            pltpu.VMEM((2, FF, 256), BF),
            pltpu.VMEM((TOK, HALF), BF),
            pltpu.VMEM((FF, TOK), BF),
            pltpu.VMEM((FF, TOK), BF),
            pltpu.SemaphoreType.DMA((n_copies,)),
            pltpu.SemaphoreType.DMA((n_copies,)),
            pltpu.SemaphoreType.DMA((4,)),
            pltpu.SemaphoreType.DMA((7,)),
        ],
        compiler_params=pltpu.CompilerParams(
            collective_id=0, has_side_effects=True, vmem_limit_bytes=64 * 2**20
        ),
        cost_estimate=pl.CostEstimate(flops=flops, bytes_accessed=2**24, transcendentals=0),
    )(gate_pre.T, up_pre.T, w_down, cotangent)
    return layer_out, grad_gate.T, grad_up.T, grad_down


def solution(mesh):
    placed = (P("dp", "tensor"), P("dp", "tensor"), P("tensor", "dp"), P("dp", "tensor"))
    return jax.shard_map(
        shards,
        mesh=mesh,
        in_specs=placed,
        out_specs=(P("dp", "tensor"), P("dp", "tensor"), P("dp", "tensor"), P("tensor", "dp")),
        check_vma=False,
    )
```

```python
import jax
import jax.numpy as jnp
from jax import lax
from jax.experimental import pallas as pl
from jax.experimental.pallas import tpu as pltpu
from jax.sharding import PartitionSpec as P

MESH = pl.DeviceIdType.MESH
BF = jnp.bfloat16
F32 = jnp.float32

TOK = 512
FF = 928
DM = 1024
HALF = 512
CUT = 464
C = 2
RC = HALF // C
HC = RC // 2


class Copies:
    def __init__(self, send, recv):
        self.send, self.recv, self.all, self.n = send, recv, [], 0

    def put(self, src, dst, target, landing=None):
        k = self.n
        self.n += 1
        copy = pltpu.make_async_remote_copy(
            src, dst, self.send.at[k], self.recv.at[k], device_id=target, device_id_type=MESH
        )
        copy.start()
        self.all.append((None, copy))
        if landing is None:
            return copy
        return pltpu.make_async_remote_copy(
            src, landing, self.send.at[k], self.recv.at[k], device_id=target, device_id_type=MESH
        )

    def put_or_keep(self, keep, src, dst, target, landing):
        k = self.n
        self.n += 1
        copy = pltpu.make_async_remote_copy(
            src, dst, self.send.at[k], self.recv.at[k], device_id=target, device_id_type=MESH
        )
        own = pltpu.make_async_copy(src, dst, self.recv.at[k])
        pl.when(keep)(own.start)
        pl.when(jnp.logical_not(keep))(copy.start)
        self.all.append((keep, copy))
        got = pltpu.make_async_remote_copy(
            src, landing, self.send.at[k], self.recv.at[k], device_id=target, device_id_type=MESH
        )

        def wait():
            pl.when(keep)(own.wait)
            pl.when(jnp.logical_not(keep))(got.wait_recv)

        return wait

    def finish(self):
        for keep, copy in self.all:
            if keep is None:
                copy.wait_send()
            else:
                pl.when(jnp.logical_not(keep))(copy.wait_send)


def nn(a, b):
    return lax.dot_general(a, b, (((1,), (0,)), ((), ())), preferred_element_type=F32)


def nt(a, b):
    return lax.dot_general(a, b, (((1,), (1,)), ((), ())), preferred_element_type=F32)


def kernel(
    gate_in, up_in, w_in, cot_in, lay_out, gg_out, gu_out, gd_out,
    gate, up, w, cot, HT, CT, WT, OWN, ZM, G, R1, R3, RAB, RO, LO, LS, LX, LH, LD, LY, FIN, SWP,
    acc, gd_stage, lay_stage, gg_stage, gu_stage, send_sem, recv_sem, in_sem, out_sem,
):
    dp, t = lax.axis_index("dp"), lax.axis_index("tensor")
    x, yl = dp // 2, dp % 2
    yh, z, c = t // 8, (t // 2) % 4, t % 2
    j = t // 2

    def X(d):
        return (((x + d + 4) % 4) * 2 + yl, t)

    def Z(d):
        return (dp, yh * 8 + ((z + d + 4) % 4) * 2 + c)

    YL = (x * 2 + 1 - yl, t)
    YH = (dp, (1 - yh) * 8 + z * 2 + c)
    CORE = (dp, t + 1 - 2 * c)
    x1, x0, z1, z0 = x // 2, x % 2, z // 2, z % 2
    T1, T1S, T2, SW, SWS, q = [], [], [], [], [], []
    for k in range(C):
        there = ((yl + yh + z0) % 2) * 8 + (2 * ((x1 + yh + k) % 2) + (x0 + z1) % 2) * 2 + c
        T1.append((x * 2 + z0, there))
        hi, lo = (z1 + x1 + k) % 2, (z0 + x0) % 2
        T1S.append((x * 2 + (yh + hi + yl) % 2, hi * 8 + (2 * lo + yl) * 2 + c))
        T2.append(((2 * hi + lo) * 2 + yl, t))
        q.append((2 * hi + lo) * 2 + (yh + x1 + yl) % 2)
        SW.append((q[k], 2 * dp + c))
        SWS.append((j, there))

    def here(device):
        return jnp.logical_and(device[0] == dp, device[1] == t)

    def tok(dx, other):
        row = 1 - yl if other else yl
        return ((x + dx + 4) % 4) * 2 + row

    def place(dz, other, k):
        row, at = (1 - yh if other else yh), (z + dz + 4) % 4
        return (2 * ((at // 2 + x1 + k) % 2) + (at + x0) % 2) * 2 + (row + x1 + yl) % 2

    barrier = pltpu.get_barrier_semaphore()
    greeted = (X(1), X(-1), YL, Z(1), Z(-1), YH, CORE, *T1, *T1S, *T2, *SW, *SWS)
    for other in greeted:
        pl.semaphore_signal(barrier, inc=1, device_id=other, device_id_type=MESH)
    loads = []
    for n, (src, dst) in enumerate(((cot_in, cot), (gate_in, gate), (up_in, up), (w_in, w))):
        loads.append(pltpu.make_async_copy(src, dst, in_sem.at[n]))
        loads[-1].start()

    loads[0].wait()
    for r in range(0, HALF, 128):
        OWN[:, r : r + 128] = cot[r : r + 128, :].astype(F32).T.astype(BF)
    loads[1].wait()
    loads[2].wait()

    def make_hidden(k, _):
        rows = pl.ds(pl.multiple_of(k * 32, 32), 32)
        g = gate[rows, :].astype(F32)
        HT[dp, rows, :] = (g * jax.nn.sigmoid(g) * up[rows, :].astype(F32)).astype(BF)
        return 0

    pl.semaphore_wait(barrier, len(greeted))
    cp = Copies(send_sem, recv_sem)
    low, high = pl.ds(0, CUT), pl.ds(CUT, FF - CUT)

    def crow(k, size=RC):
        return pl.ds(pl.multiple_of(c * HALF + k, 16), size)

    def share(ref, target):
        return cp.put(ref, ref, target)

    t1, t2 = [], []
    for k in range(C):
        at = pl.ds(k * RC, RC)
        t1.append(cp.put_or_keep(here(T1[k]), OWN.at[at], ZM.at[at], T1[k], ZM.at[at]))
    lax.fori_loop(0, 29, make_hidden, 0)
    s1p, s1m = [share(HT.at[dp, low], X(1))], [share(HT.at[dp, high], X(-1))]
    s1y = share(HT.at[dp], YL)

    loads[3].wait()
    for r in range(0, FF, CUT):
        WT[:, r : r + CUT] = w[r : r + CUT, :].astype(F32).T.astype(BF)

    for k in range(C):
        t1[k]()
        t2.append(cp.put_or_keep(here(T2[k]), ZM.at[pl.ds(k * RC, RC)], CT.at[T1S[k][0], crow(k * RC)], T2[k], CT.at[q[k], crow(k * RC)]))

    def make_layer(g):
        def part(k, _):
            cols = pl.ds(pl.multiple_of(k * 256, 256), 256)
            here = pl.ds(pl.multiple_of(c * HALF, HALF), HALF)
            there = pl.ds(pl.multiple_of((1 - c) * HALF, HALF), HALF)
            h = HT[g, :, cols]
            LS[g, :, cols] = nn(WT[there, :], h).astype(BF)
            LO[g, :, cols] = nn(WT[here, :], h).astype(BF)
            return 0

        lax.fori_loop(0, 2, part, 0)
        return cp.put(LS.at[g], LX.at[g], CORE)

    lx = [make_layer(dp)]

    s1p[0].wait_recv()
    s1m[0].wait_recv()
    s2 = [share(HT.at[tok(-1, False), low], X(1)), share(HT.at[tok(1, False), high], X(-1))]
    s1p.append(share(HT.at[dp, high], X(1)))
    s1m.append(share(HT.at[dp, low], X(-1)))

    def spread(row, k):
        ref = CT.at[place(0, row, k), crow(k * RC)]
        return share(ref, Z(1)), share(ref, Z(-1))

    def forward(row, k):
        a = CT.at[place(-1, row, k), crow(k * RC, HC)]
        b = CT.at[place(1, row, k), crow(k * RC + HC, HC)]
        return share(a, Z(1)), share(b, Z(-1))

    t3, t5, near = [], [], {}

    def cross(dz, row, k):
        t5.append(share(CT.at[place(dz, row, k), crow(k * RC)], CORE))

    for k in range(C):
        t2[k]()
        t3.append(share(CT.at[q[k], crow(k * RC)], YH))
        near[False, k] = spread(False, k)
        cross(0, False, k)
    s1y.wait_recv()
    par = HT.at[tok(0, True)]
    s3p, s3m = share(par, X(1)), share(par, X(-1))

    for k in range(C):
        t3[k].wait_recv()
        near[True, k] = spread(True, k)
        cross(0, True, k)
    s2[0].wait_recv()
    s2[1].wait_recv()
    s4 = share(HT.at[tok(2, False)], YL)
    lx.append(make_layer(tok(0, True)))
    lx.append(make_layer(tok(2, False)))

    far = {}
    for row in (False, True):
        for k in range(C):
            near[row, k][0].wait_recv()
            near[row, k][1].wait_recv()
            far[row, k] = forward(row, k)
            cross(1, row, k)
            cross(-1, row, k)
    s1p[1].wait_recv()
    s1m[1].wait_recv()
    lx.append(make_layer(tok(1, False)))
    lx.append(make_layer(tok(-1, False)))
    for row in (False, True):
        for k in range(C):
            far[row, k][0].wait_recv()
            far[row, k][1].wait_recv()
            cross(2, row, k)
    for f in t5:
        f.wait_recv()

    def make_grad(g):
        def part(k, _):
            cols = pl.ds(pl.multiple_of(k * 256, 256), 256)
            G[g, :, cols] = nn(w[...], CT[g, :, cols]).astype(BF)
            return 0

        lax.fori_loop(0, 2, part, 0)

    make_grad(tok(2, True))
    g1 = cp.put(G.at[tok(2, True)], R1, YL)
    make_grad(tok(1, True))
    g3p = cp.put(G.at[tok(1, True)], R3.at[0], X(1))
    make_grad(tok(-1, True))
    g3m = cp.put(G.at[tok(-1, True)], R3.at[1], X(-1))
    s4.wait_recv()
    lx.append(make_layer(tok(2, True)))
    s3p.wait_recv()
    lx.append(make_layer(tok(-1, True)))
    s3m.wait_recv()
    lx.append(make_layer(tok(1, True)))
    for f in lx:
        f.wait_recv()

    def pair(dz, row, k):
        block, at = place(dz, row, k), pl.ds(k * RC, RC)
        LO[block, at] = (LO[block, at].astype(F32) + LX[block, at].astype(F32)).astype(BF)

    halves, directs = {}, {}
    rows = ((0, True), (1, False))
    for n, row in rows:
        for k in range(C):
            pair(2, row, k)
            two = place(2, row, k)
            halves[n, k] = (
                cp.put(LO.at[two, pl.ds(k * RC, HC)], LH.at[n, 0, k], Z(1)),
                cp.put(LO.at[two, pl.ds(k * RC + HC, HC)], LH.at[n, 1, k], Z(-1)),
            )
    for n, row in rows:
        for k in range(C):
            pair(1, row, k)
            pair(-1, row, k)

    def relay(n, row, k):
        sent = []
        for side, dz in ((0, 1), (1, -1)):
            block = place(dz, row, k)
            halves[n, k][side].wait_recv()
            at = pl.ds(k * RC + side * HC, HC)
            LO[block, at] = (LO[block, at].astype(F32) + LH[n, side, k].astype(F32)).astype(BF)
            at = pl.ds(k * RC, RC)
            sent.append(cp.put(LO.at[block, at], LD.at[n, side, at], Z(dz)))
        directs[n, k] = sent

    make_grad(tok(2, False))
    for n, row in rows:
        for k in range(C):
            relay(n, row, k)
        if row:
            make_grad(tok(1, False))
            make_grad(tok(-1, False))

    def weight_grad(n):
        cols = pl.ds(n * 256, 256)
        acc[...] = jnp.zeros_like(acc)

        def add(g, _):
            acc[...] += nt(HT[g], CT[g, cols, :])
            return 0

        lax.fori_loop(0, 8, add, 0)
        gd_stage[n % 2] = acc[...].astype(BF)
        copy = pltpu.make_async_copy(gd_stage.at[n % 2], gd_out.at[:, cols], out_sem.at[n])
        copy.start()
        return copy

    g1.wait_recv()
    two = tok(2, False)
    G[two] = (G[two].astype(F32) + R1[...].astype(F32)).astype(BF)
    g2a = cp.put(G.at[two, low], RAB.at[low], X(1))
    g2b = cp.put(G.at[two, high], RAB.at[high], X(-1))
    up_one, down_one = tok(1, False), tok(-1, False)
    g5 = [cp.put(G.at[up_one, high], RO.at[0, high], X(1)), cp.put(G.at[down_one, low], RO.at[1, low], X(-1))]
    for k in range(C):
        pair(0, True, k)
        pair(0, False, k)
    make_grad(tok(0, True))

    ly, outs = [], []
    for k in range(C):
        block = place(0, True, k)
        at = pl.ds(k * RC, RC)
        directs[0, k][0].wait_recv()
        directs[0, k][1].wait_recv()
        LO[block, at] = (
            LO[block, at].astype(F32) + LD[0, 0, at].astype(F32) + LD[0, 1, at].astype(F32)
        ).astype(BF)
        ly.append(cp.put(LO.at[block, at], LY.at[at], YH))
        if k == 0:
            make_grad(dp)
    g3p.wait_recv()
    g3m.wait_recv()
    par = tok(0, True)
    G[par] = (G[par].astype(F32) + R3[0].astype(F32) + R3[1].astype(F32)).astype(BF)
    g5.append(cp.put(G.at[par], RO.at[2], YL))

    outs.append(weight_grad(0))
    outs.append(weight_grad(1))

    sw = []
    for k in range(C):
        at = pl.ds(k * RC, RC)
        directs[1, k][0].wait_recv()
        directs[1, k][1].wait_recv()
        ly[k].wait_recv()
        FIN[at] = (
            LO[q[k], at].astype(F32) + LD[1, 0, at].astype(F32) + LD[1, 1, at].astype(F32) + LY[at].astype(F32)
        ).astype(BF)
        sw.append(cp.put_or_keep(here(SW[k]), FIN.at[at], SWP.at[at], SW[k], SWP.at[at]))

    g2a.wait_recv()
    G[up_one, low] = (G[up_one, low].astype(F32) + RAB[low].astype(F32)).astype(BF)
    g5.append(cp.put(G.at[up_one, low], RO.at[0, low], X(1)))
    g2b.wait_recv()
    G[down_one, high] = (G[down_one, high].astype(F32) + RAB[high].astype(F32)).astype(BF)
    g5.append(cp.put(G.at[down_one, high], RO.at[1, high], X(-1)))

    outs[0].wait()
    outs.append(weight_grad(2))
    outs[1].wait()
    outs.append(weight_grad(3))

    for k in range(C):
        sw[k]()
        at = pl.ds(k * RC, RC)
        for r in range(0, TOK, 128):
            lay_stage[r : r + 128, k * RC : (k + 1) * RC] = SWP[at, r : r + 128].astype(F32).T.astype(BF)
    copy = pltpu.make_async_copy(lay_stage, lay_out, out_sem.at[4])
    copy.start()
    outs.append(copy)

    for f in g5:
        f.wait_recv()

    def finish(k, _):
        rows = pl.ds(pl.multiple_of(k * 32, 32), 32)
        total = G[dp, rows, :].astype(F32)
        for side in range(3):
            total = total + RO[side, rows, :].astype(F32)
        g = gate[rows, :].astype(F32)
        squash = jax.nn.sigmoid(g)
        gu_stage[rows, :] = (total * g * squash).astype(BF)
        gg_stage[rows, :] = (
            total * up[rows, :].astype(F32) * squash * (1.0 + g * (1.0 - squash))
        ).astype(BF)
        return 0

    lax.fori_loop(0, 29, finish, 0)
    for n, (stage, out) in enumerate(((gg_stage, gg_out), (gu_stage, gu_out))):
        copy = pltpu.make_async_copy(stage, out, out_sem.at[5 + n])
        copy.start()
        outs.append(copy)
    cp.finish()
    for copy in outs[2:]:
        copy.wait()


def place_outputs(*refs):
    sources, results, stages, sems = refs[:4], refs[4:8], refs[8:12], refs[12]
    arrive = [pltpu.make_async_copy(sources[n], stages[n], sems.at[n]) for n in range(4)]
    leave = [pltpu.make_async_copy(stages[n], results[n], sems.at[4 + n]) for n in range(4)]
    for copy in arrive:
        copy.start()
    for n in range(4):
        arrive[n].wait()
        leave[n].start()
    for copy in leave:
        copy.wait()


def shards(gate_pre, up_pre, w_down, cotangent):
    anywhere = pl.BlockSpec(memory_space=pl.ANY)
    n_copies = 100
    flops = 2 * 3 * TOK * FF * 8192
    shapes = (
        jax.ShapeDtypeStruct((TOK, HALF), BF),
        jax.ShapeDtypeStruct((FF, TOK), BF),
        jax.ShapeDtypeStruct((FF, TOK), BF),
        jax.ShapeDtypeStruct((FF, DM), BF),
    )
    results = pl.pallas_call(
        kernel,
        out_shape=shapes,
        in_specs=[anywhere] * 4,
        out_specs=[anywhere] * 4,
        scratch_shapes=[
            pltpu.VMEM((FF, TOK), BF),
            pltpu.VMEM((FF, TOK), BF),
            pltpu.VMEM((FF, DM), BF),
            pltpu.VMEM((TOK, HALF), BF),
            pltpu.VMEM((8, FF, TOK), BF),
            pltpu.VMEM((8, DM, TOK), BF),
            pltpu.VMEM((DM, FF), BF),
            pltpu.VMEM((HALF, TOK), BF),
            pltpu.VMEM((HALF, TOK), BF),
            pltpu.VMEM((8, FF, TOK), BF),
            pltpu.VMEM((FF, TOK), BF),
            pltpu.VMEM((2, FF, TOK), BF),
            pltpu.VMEM((FF, TOK), BF),
            pltpu.VMEM((3, FF, TOK), BF),
            pltpu.VMEM((8, HALF, TOK), BF),
            pltpu.VMEM((8, HALF, TOK), BF),
            pltpu.VMEM((8, HALF, TOK), BF),
            pltpu.VMEM((2, 2, C, HC, TOK), BF),
            pltpu.VMEM((2, 2, HALF, TOK), BF),
            pltpu.VMEM((HALF, TOK), BF),
            pltpu.VMEM((HALF, TOK), BF),
            pltpu.VMEM((HALF, TOK), BF),
            pltpu.VMEM((FF, 256), F32),
            pltpu.VMEM((2, FF, 256), BF),
            pltpu.VMEM((TOK, HALF), BF),
            pltpu.VMEM((FF, TOK), BF),
            pltpu.VMEM((FF, TOK), BF),
            pltpu.SemaphoreType.DMA((n_copies,)),
            pltpu.SemaphoreType.DMA((n_copies,)),
            pltpu.SemaphoreType.DMA((4,)),
            pltpu.SemaphoreType.DMA((7,)),
        ],
        compiler_params=pltpu.CompilerParams(
            collective_id=0, has_side_effects=True, vmem_limit_bytes=64 * 2**20
        ),
        cost_estimate=pl.CostEstimate(flops=flops, bytes_accessed=2**24, transcendentals=0),
    )(gate_pre.T, up_pre.T, w_down, cotangent)
    layer_out, grad_gate, grad_up, grad_down = pl.pallas_call(
        place_outputs,
        out_shape=shapes,
        in_specs=[anywhere] * 4,
        out_specs=[anywhere] * 4,
        scratch_shapes=[pltpu.VMEM(shape.shape, BF) for shape in shapes] + [pltpu.SemaphoreType.DMA((8,))],
        compiler_params=pltpu.CompilerParams(vmem_limit_bytes=64 * 2**20),
    )(*results)
    return layer_out, grad_gate.T, grad_up.T, grad_down


def solution(mesh):
    placed = (P("dp", "tensor"), P("dp", "tensor"), P("tensor", "dp"), P("dp", "tensor"))
    return jax.shard_map(
        shards,
        mesh=mesh,
        in_specs=placed,
        out_specs=(P("dp", "tensor"), P("dp", "tensor"), P("dp", "tensor"), P("tensor", "dp")),
        check_vma=False,
    )
```

```python
import jax
import jax.numpy as jnp
from jax import lax
from jax.experimental import pallas as pl
from jax.experimental.pallas import tpu as pltpu
from jax.sharding import PartitionSpec as P

MESH = pl.DeviceIdType.MESH
BF = jnp.bfloat16
F32 = jnp.float32

TOK = 512
FF = 928
DM = 1024
HALF = 512
SIDE = 96
CUT = 464
C = 2
RC = HALF // C
HC = RC // 2


class Copies:
    def __init__(self, send, recv):
        self.send, self.recv, self.all, self.n = send, recv, [], 0

    def put(self, src, dst, target, landing=None):
        k = self.n
        self.n += 1
        copy = pltpu.make_async_remote_copy(
            src, dst, self.send.at[k], self.recv.at[k], device_id=target, device_id_type=MESH
        )
        copy.start()
        self.all.append((None, copy))
        if landing is None:
            return copy
        return pltpu.make_async_remote_copy(
            src, landing, self.send.at[k], self.recv.at[k], device_id=target, device_id_type=MESH
        )

    def put_or_keep(self, keep, src, dst, target, landing):
        k = self.n
        self.n += 1
        copy = pltpu.make_async_remote_copy(
            src, dst, self.send.at[k], self.recv.at[k], device_id=target, device_id_type=MESH
        )
        own = pltpu.make_async_copy(src, dst, self.recv.at[k])
        pl.when(keep)(own.start)
        pl.when(jnp.logical_not(keep))(copy.start)
        self.all.append((keep, copy))
        got = pltpu.make_async_remote_copy(
            src, landing, self.send.at[k], self.recv.at[k], device_id=target, device_id_type=MESH
        )

        def wait():
            pl.when(keep)(own.wait)
            pl.when(jnp.logical_not(keep))(got.wait_recv)

        return wait

    def finish(self):
        for keep, copy in self.all:
            if keep is None:
                copy.wait_send()
            else:
                pl.when(jnp.logical_not(keep))(copy.wait_send)


def nn(a, b):
    return lax.dot_general(a, b, (((1,), (0,)), ((), ())), preferred_element_type=F32)


def nt(a, b):
    return lax.dot_general(a, b, (((1,), (1,)), ((), ())), preferred_element_type=F32)


def kernel(
    gate_in, up_in, w_in, cot_in, lay_out, gg_out, gu_out, gd_out,
    gate, up, w, cot, HT, CT, WT, OWN, ZM, G, R1, R3, RAB, RO, LO, LS, LX, LH, LD, LY, FIN, SWP,
    acc, gd_stage, lay_stage, gg_stage, gu_stage, send_sem, recv_sem, in_sem, out_sem,
):
    dp, t = lax.axis_index("dp"), lax.axis_index("tensor")
    x, yl = dp // 2, dp % 2
    yh, z, c = t // 8, (t // 2) % 4, t % 2
    j = t // 2

    def X(d):
        return (((x + d + 4) % 4) * 2 + yl, t)

    def Z(d):
        return (dp, yh * 8 + ((z + d + 4) % 4) * 2 + c)

    YL = (x * 2 + 1 - yl, t)
    YH = (dp, (1 - yh) * 8 + z * 2 + c)
    CORE = (dp, t + 1 - 2 * c)
    x1, x0, z1, z0 = x // 2, x % 2, z // 2, z % 2
    T1, T1S, T2, SW, SWS, q = [], [], [], [], [], []
    for k in range(C):
        there = ((yl + yh + z0) % 2) * 8 + (2 * ((x1 + yh + k) % 2) + (x0 + z1) % 2) * 2 + c
        T1.append((x * 2 + z0, there))
        hi, lo = (z1 + x1 + k) % 2, (z0 + x0) % 2
        T1S.append((x * 2 + (yh + hi + yl) % 2, hi * 8 + (2 * lo + yl) * 2 + c))
        T2.append(((2 * hi + lo) * 2 + yl, t))
        q.append((2 * hi + lo) * 2 + (yh + x1 + yl) % 2)
        SW.append((q[k], 2 * dp + c))
        SWS.append((j, there))

    def here(device):
        return jnp.logical_and(device[0] == dp, device[1] == t)

    def tok(dx, other):
        row = 1 - yl if other else yl
        return ((x + dx + 4) % 4) * 2 + row

    def place(dz, other, k):
        row, at = (1 - yh if other else yh), (z + dz + 4) % 4
        return (2 * ((at // 2 + x1 + k) % 2) + (at + x0) % 2) * 2 + (row + x1 + yl) % 2

    barrier = pltpu.get_barrier_semaphore()
    greeted = (X(1), X(-1), YL, Z(1), Z(-1), YH, CORE, *T1, *T1S, *T2, *SW, *SWS)
    for other in greeted:
        pl.semaphore_signal(barrier, inc=1, device_id=other, device_id_type=MESH)
    loads = []
    for n, (src, dst) in enumerate(((gate_in, gate), (up_in, up), (cot_in, cot), (w_in, w))):
        loads.append(pltpu.make_async_copy(src, dst, in_sem.at[n]))
        loads[-1].start()

    def make_hidden(k, _):
        rows = pl.ds(pl.multiple_of(k * 32, 32), 32)
        g = gate[rows, :].astype(F32)
        HT[dp, rows, :] = (g * jax.nn.sigmoid(g) * up[rows, :].astype(F32)).astype(BF)
        return 0

    loads[0].wait()
    loads[1].wait()
    lax.fori_loop(0, 29, make_hidden, 0)
    loads[2].wait()
    for r in range(0, HALF, 128):
        OWN[:, r : r + 128] = cot[r : r + 128, :].astype(F32).T.astype(BF)

    pl.semaphore_wait(barrier, len(greeted))
    cp = Copies(send_sem, recv_sem)
    low, high = pl.ds(0, CUT), pl.ds(CUT, FF - CUT)
    most, side = pl.ds(0, FF - SIDE), pl.ds(FF - SIDE, SIDE)

    def crow(k, size=RC):
        return pl.ds(pl.multiple_of(c * HALF + k, 16), size)

    def share(ref, target):
        return cp.put(ref, ref, target)

    t1, t2 = [], []
    for k in range(C):
        at = pl.ds(k * RC, RC)
        t1.append(cp.put_or_keep(here(T1[k]), OWN.at[at], ZM.at[at], T1[k], ZM.at[at]))
    s1p, s1m = [share(HT.at[dp, low], X(1))], [share(HT.at[dp, high], X(-1))]
    s1y = share(HT.at[dp], YL)

    loads[3].wait()
    for r in range(0, FF, CUT):
        WT[:, r : r + CUT] = w[r : r + CUT, :].astype(F32).T.astype(BF)

    for k in range(C):
        t1[k]()
        t2.append(cp.put_or_keep(here(T2[k]), ZM.at[pl.ds(k * RC, RC)], CT.at[T1S[k][0], crow(k * RC)], T2[k], CT.at[q[k], crow(k * RC)]))

    def make_layer(g):
        def part(k, _):
            cols = pl.ds(pl.multiple_of(k * 256, 256), 256)
            here = pl.ds(pl.multiple_of(c * HALF, HALF), HALF)
            there = pl.ds(pl.multiple_of((1 - c) * HALF, HALF), HALF)
            h = HT[g, :, cols]
            LS[g, :, cols] = nn(WT[there, :], h).astype(BF)
            LO[g, :, cols] = nn(WT[here, :], h).astype(BF)
            return 0

        lax.fori_loop(0, 2, part, 0)
        return cp.put(LS.at[g], LX.at[g], CORE)

    lx = [make_layer(dp)]

    s1p[0].wait_recv()
    s1m[0].wait_recv()
    s2 = [share(HT.at[tok(-1, False), low], X(1)), share(HT.at[tok(1, False), high], X(-1))]
    s1p.append(share(HT.at[dp, high], X(1)))
    s1m.append(share(HT.at[dp, low], X(-1)))

    def spread(row, k):
        ref = CT.at[place(0, row, k), crow(k * RC)]
        return share(ref, Z(1)), share(ref, Z(-1))

    def forward(row, k):
        a = CT.at[place(-1, row, k), crow(k * RC, HC)]
        b = CT.at[place(1, row, k), crow(k * RC + HC, HC)]
        return share(a, Z(1)), share(b, Z(-1))

    t3, t5, near = [], [], {}

    def cross(dz, row, k):
        t5.append(share(CT.at[place(dz, row, k), crow(k * RC)], CORE))

    for k in range(C):
        t2[k]()
        t3.append(share(CT.at[q[k], crow(k * RC)], YH))
        near[False, k] = spread(False, k)
        cross(0, False, k)
    s1y.wait_recv()
    par = HT.at[tok(0, True), most]
    s3p, s3m = share(par, X(1)), share(par, X(-1))

    for k in range(C):
        t3[k].wait_recv()
        near[True, k] = spread(True, k)
        cross(0, True, k)
    s2[0].wait_recv()
    s2[1].wait_recv()
    s4 = share(HT.at[tok(2, False)], YL)
    lx.append(make_layer(tok(0, True)))
    lx.append(make_layer(tok(2, False)))

    far = {}
    for row in (False, True):
        for k in range(C):
            near[row, k][0].wait_recv()
            near[row, k][1].wait_recv()
            far[row, k] = forward(row, k)
            cross(1, row, k)
            cross(-1, row, k)
    s1p[1].wait_recv()
    s1m[1].wait_recv()
    s6 = [share(HT.at[tok(dx, False), side], YL) for dx in (1, -1)]
    lx.append(make_layer(tok(1, False)))
    lx.append(make_layer(tok(-1, False)))
    for row in (False, True):
        for k in range(C):
            far[row, k][0].wait_recv()
            far[row, k][1].wait_recv()
            cross(2, row, k)
    for f in t5:
        f.wait_recv()

    def make_grad(g):
        def part(k, _):
            cols = pl.ds(pl.multiple_of(k * 256, 256), 256)
            G[g, :, cols] = nn(w[...], CT[g, :, cols]).astype(BF)
            return 0

        lax.fori_loop(0, 2, part, 0)

    make_grad(tok(2, True))
    g1 = cp.put(G.at[tok(2, True)], R1, YL)
    make_grad(tok(1, True))
    g3p = cp.put(G.at[tok(1, True), most], R3.at[0, most], X(1))
    make_grad(tok(-1, True))
    g3m = cp.put(G.at[tok(-1, True), most], R3.at[1, most], X(-1))
    g6 = [cp.put(G.at[tok(dx, True), side], R3.at[n, side], YL) for n, dx in enumerate((1, -1))]
    s4.wait_recv()
    lx.append(make_layer(tok(2, True)))
    s3p.wait_recv()
    s6[1].wait_recv()
    lx.append(make_layer(tok(-1, True)))
    s3m.wait_recv()
    s6[0].wait_recv()
    lx.append(make_layer(tok(1, True)))
    for f in lx:
        f.wait_recv()

    def pair(dz, row, k):
        block, at = place(dz, row, k), pl.ds(k * RC, RC)
        LO[block, at] = (LO[block, at].astype(F32) + LX[block, at].astype(F32)).astype(BF)

    halves, directs = {}, {}
    rows = ((0, True), (1, False))
    for n, row in rows:
        for k in range(C):
            pair(2, row, k)
            two = place(2, row, k)
            halves[n, k] = (
                cp.put(LO.at[two, pl.ds(k * RC, HC)], LH.at[n, 0, k], Z(1)),
                cp.put(LO.at[two, pl.ds(k * RC + HC, HC)], LH.at[n, 1, k], Z(-1)),
            )
    for n, row in rows:
        for k in range(C):
            pair(1, row, k)
            pair(-1, row, k)

    def relay(n, row, k):
        sent = []
        for side, dz in ((0, 1), (1, -1)):
            block = place(dz, row, k)
            halves[n, k][side].wait_recv()
            at = pl.ds(k * RC + side * HC, HC)
            LO[block, at] = (LO[block, at].astype(F32) + LH[n, side, k].astype(F32)).astype(BF)
            at = pl.ds(k * RC, RC)
            sent.append(cp.put(LO.at[block, at], LD.at[n, side, at], Z(dz)))
        directs[n, k] = sent

    make_grad(tok(2, False))
    for n, row in rows:
        for k in range(C):
            relay(n, row, k)
        if row:
            make_grad(tok(1, False))
            make_grad(tok(-1, False))

    def weight_grad(n):
        cols = pl.ds(n * 256, 256)
        acc[...] = jnp.zeros_like(acc)

        def add(g, _):
            acc[...] += nt(HT[g], CT[g, cols, :])
            return 0

        lax.fori_loop(0, 8, add, 0)
        gd_stage[n % 2] = acc[...].astype(BF)
        copy = pltpu.make_async_copy(gd_stage.at[n % 2], gd_out.at[:, cols], out_sem.at[n])
        copy.start()
        return copy

    g1.wait_recv()
    two = tok(2, False)
    G[two] = (G[two].astype(F32) + R1[...].astype(F32)).astype(BF)
    g2a = cp.put(G.at[two, low], RAB.at[low], X(1))
    g2b = cp.put(G.at[two, high], RAB.at[high], X(-1))
    up_one, down_one = tok(1, False), tok(-1, False)
    for n, block in enumerate((up_one, down_one)):
        g6[n].wait_recv()
        G[block, side] = (G[block, side].astype(F32) + R3[n, side].astype(F32)).astype(BF)
    g5 = [cp.put(G.at[up_one, high], RO.at[0, high], X(1)), cp.put(G.at[down_one, low], RO.at[1, low], X(-1))]
    for k in range(C):
        pair(0, True, k)
        pair(0, False, k)
    make_grad(tok(0, True))

    ly, outs = [], []
    for k in range(C):
        block = place(0, True, k)
        at = pl.ds(k * RC, RC)
        directs[0, k][0].wait_recv()
        directs[0, k][1].wait_recv()
        LO[block, at] = (
            LO[block, at].astype(F32) + LD[0, 0, at].astype(F32) + LD[0, 1, at].astype(F32)
        ).astype(BF)
        ly.append(cp.put(LO.at[block, at], LY.at[at], YH))
        if k == 0:
            make_grad(dp)
    g3p.wait_recv()
    g3m.wait_recv()
    par = tok(0, True)
    G[par, most] = (G[par, most].astype(F32) + R3[0, most].astype(F32) + R3[1, most].astype(F32)).astype(BF)
    g5.append(cp.put(G.at[par], RO.at[2], YL))

    g2a.wait_recv()
    G[up_one, low] = (G[up_one, low].astype(F32) + RAB[low].astype(F32)).astype(BF)
    g2b.wait_recv()
    G[down_one, high] = (G[down_one, high].astype(F32) + RAB[high].astype(F32)).astype(BF)

    def last(part):
        at = pl.ds(*((0, 256) if part == 0 else (256, CUT - 256)))
        g5.append(cp.put(G.at[up_one, at], RO.at[0, at], X(1)))
        at = pl.ds(*((CUT, 256) if part == 0 else (CUT + 256, FF - CUT - 256)))
        g5.append(cp.put(G.at[down_one, at], RO.at[1, at], X(-1)))

    last(0)
    outs.append(weight_grad(0))
    outs.append(weight_grad(1))

    sw = []
    for k in range(C):
        at = pl.ds(k * RC, RC)
        directs[1, k][0].wait_recv()
        directs[1, k][1].wait_recv()
        ly[k].wait_recv()
        FIN[at] = (
            LO[q[k], at].astype(F32) + LD[1, 0, at].astype(F32) + LD[1, 1, at].astype(F32) + LY[at].astype(F32)
        ).astype(BF)
        sw.append(cp.put_or_keep(here(SW[k]), FIN.at[at], SWP.at[at], SW[k], SWP.at[at]))

    last(1)
    outs[0].wait()
    outs.append(weight_grad(2))
    outs[1].wait()
    outs.append(weight_grad(3))

    for k in range(C):
        sw[k]()
        at = pl.ds(k * RC, RC)
        for r in range(0, TOK, 128):
            lay_stage[r : r + 128, k * RC : (k + 1) * RC] = SWP[at, r : r + 128].astype(F32).T.astype(BF)
    copy = pltpu.make_async_copy(lay_stage, lay_out, out_sem.at[4])
    copy.start()
    outs.append(copy)

    def finish(k, _):
        rows = pl.ds(pl.multiple_of(k * 16, 16), 16)
        total = G[dp, rows, :].astype(F32)
        for n in range(3):
            total = total + RO[n, rows, :].astype(F32)
        g = gate[rows, :].astype(F32)
        squash = jax.nn.sigmoid(g)
        gu_stage[rows, :] = (total * g * squash).astype(BF)
        gg_stage[rows, :] = (
            total * up[rows, :].astype(F32) * squash * (1.0 + g * (1.0 - squash))
        ).astype(BF)
        return 0

    n = 5
    for part, spans in enumerate((((0, 256), (CUT, CUT + 256)), ((256, CUT), (CUT + 256, FF)))):
        for f in g5[:5] if part == 0 else g5[5:]:
            f.wait_recv()
        for start, end in spans:
            lax.fori_loop(start // 16, end // 16, finish, 0, unroll=2 if part == 0 else 1)
            for stage, out in ((gg_stage, gg_out), (gu_stage, gu_out)):
                at = pl.ds(start, end - start)
                copy = pltpu.make_async_copy(stage.at[at], out.at[at], out_sem.at[n])
                copy.start()
                outs.append(copy)
                n += 1
    cp.finish()
    for copy in outs[2:]:
        copy.wait()


def place_outputs(*refs):
    sources, results, stages, sems = refs[:4], refs[4:8], refs[8:12], refs[12]
    arrive, leave = [], []
    for n in (0, 3, 1, 2):
        rows = sources[n].shape[0] // 2
        for part in range(2):
            at, k = pl.ds(part * rows, rows), len(arrive)
            arrive.append(pltpu.make_async_copy(sources[n].at[at], stages[n].at[at], sems.at[k]))
            leave.append(pltpu.make_async_copy(stages[n].at[at], results[n].at[at], sems.at[8 + k]))
    for copy in arrive:
        copy.start()
    for k in range(8):
        arrive[k].wait()
        leave[k].start()
    for copy in leave:
        copy.wait()


def shards(gate_pre, up_pre, w_down, cotangent):
    anywhere = pl.BlockSpec(memory_space=pl.ANY)
    n_copies = 100
    flops = 2 * 3 * TOK * FF * 8192
    shapes = (
        jax.ShapeDtypeStruct((TOK, HALF), BF),
        jax.ShapeDtypeStruct((FF, TOK), BF),
        jax.ShapeDtypeStruct((FF, TOK), BF),
        jax.ShapeDtypeStruct((FF, DM), BF),
    )
    results = pl.pallas_call(
        kernel,
        out_shape=shapes,
        in_specs=[anywhere] * 4,
        out_specs=[anywhere] * 4,
        scratch_shapes=[
            pltpu.VMEM((FF, TOK), BF),
            pltpu.VMEM((FF, TOK), BF),
            pltpu.VMEM((FF, DM), BF),
            pltpu.VMEM((TOK, HALF), BF),
            pltpu.VMEM((8, FF, TOK), BF),
            pltpu.VMEM((8, DM, TOK), BF),
            pltpu.VMEM((DM, FF), BF),
            pltpu.VMEM((HALF, TOK), BF),
            pltpu.VMEM((HALF, TOK), BF),
            pltpu.VMEM((8, FF, TOK), BF),
            pltpu.VMEM((FF, TOK), BF),
            pltpu.VMEM((2, FF, TOK), BF),
            pltpu.VMEM((FF, TOK), BF),
            pltpu.VMEM((3, FF, TOK), BF),
            pltpu.VMEM((8, HALF, TOK), BF),
            pltpu.VMEM((8, HALF, TOK), BF),
            pltpu.VMEM((8, HALF, TOK), BF),
            pltpu.VMEM((2, 2, C, HC, TOK), BF),
            pltpu.VMEM((2, 2, HALF, TOK), BF),
            pltpu.VMEM((HALF, TOK), BF),
            pltpu.VMEM((HALF, TOK), BF),
            pltpu.VMEM((HALF, TOK), BF),
            pltpu.VMEM((FF, 256), F32),
            pltpu.VMEM((2, FF, 256), BF),
            pltpu.VMEM((TOK, HALF), BF),
            pltpu.VMEM((FF, TOK), BF),
            pltpu.VMEM((FF, TOK), BF),
            pltpu.SemaphoreType.DMA((n_copies,)),
            pltpu.SemaphoreType.DMA((n_copies,)),
            pltpu.SemaphoreType.DMA((4,)),
            pltpu.SemaphoreType.DMA((13,)),
        ],
        compiler_params=pltpu.CompilerParams(
            collective_id=0, has_side_effects=True, vmem_limit_bytes=64 * 2**20
        ),
        cost_estimate=pl.CostEstimate(flops=flops, bytes_accessed=2**24, transcendentals=0),
    )(gate_pre.T, up_pre.T, w_down, cotangent)
    layer_out, grad_gate, grad_up, grad_down = pl.pallas_call(
        place_outputs,
        out_shape=shapes,
        in_specs=[anywhere] * 4,
        out_specs=[anywhere] * 4,
        scratch_shapes=[pltpu.VMEM(shape.shape, BF) for shape in shapes] + [pltpu.SemaphoreType.DMA((16,))],
        compiler_params=pltpu.CompilerParams(vmem_limit_bytes=64 * 2**20),
    )(*results)
    return layer_out, grad_gate.T, grad_up.T, grad_down


def solution(mesh):
    placed = (P("dp", "tensor"), P("dp", "tensor"), P("tensor", "dp"), P("dp", "tensor"))
    return jax.shard_map(
        shards,
        mesh=mesh,
        in_specs=placed,
        out_specs=(P("dp", "tensor"), P("dp", "tensor"), P("dp", "tensor"), P("tensor", "dp")),
        check_vma=False,
    )
```

```python
import jax
import jax.numpy as jnp
from jax import lax
from jax.experimental import pallas as pl
from jax.experimental.pallas import tpu as pltpu
from jax.sharding import PartitionSpec as P

MESH = pl.DeviceIdType.MESH
BF = jnp.bfloat16
F32 = jnp.float32

TOK = 512
FF = 928
DM = 1024
HALF = 512
CUT = 464
C = 4
RC = HALF // C
HC = RC // 2
CL = 2
RL = HALF // CL
HL = RL // 2


class Copies:
    def __init__(self, send, recv):
        self.send, self.recv, self.all, self.n = send, recv, [], 0

    def ids(self, count):
        self.n += count
        return self.n - count

    def put(self, src, dst, target):
        k = self.ids(1)
        copy = pltpu.make_async_remote_copy(
            src, dst, self.send.at[k], self.recv.at[k], device_id=target, device_id_type=MESH
        )
        copy.start()
        self.all.append((None, copy))
        return copy

    def put_or_keep(self, keep, src, dst, target, at=None):
        ks, kr = at or (self.ids(1),) * 2
        copy = pltpu.make_async_remote_copy(
            src, dst, self.send.at[ks], self.recv.at[kr], device_id=target, device_id_type=MESH
        )
        pl.when(keep)(pltpu.make_async_copy(src, dst, self.recv.at[kr]).start)
        pl.when(jnp.logical_not(keep))(copy.start)
        self.all.append((keep, copy))
        return ks, kr

    def landed(self, keep, src, landing, kr, target):
        got = pltpu.make_async_remote_copy(
            src, landing, self.send.at[kr], self.recv.at[kr], device_id=target, device_id_type=MESH
        )
        pl.when(keep)(pltpu.make_async_copy(src, landing, self.recv.at[kr]).wait)
        pl.when(jnp.logical_not(keep))(got.wait_recv)

    def finish(self):
        for keep, copy in self.all:
            if keep is None:
                copy.wait_send()
            else:
                pl.when(jnp.logical_not(keep))(copy.wait_send)
        self.all = []


def nn(a, b):
    return lax.dot_general(a, b, (((1,), (0,)), ((), ())), preferred_element_type=F32)


def nt(a, b):
    return lax.dot_general(a, b, (((1,), (1,)), ((), ())), preferred_element_type=F32)


def kernel(
    gate_in, up_in, w_in, cot_in, lay_out, gg_out, gu_out, gd_out,
    gate, up, cot, W2, WT, HT, CT, OWN, ZM, G, RAB, RO, LO, LS, LX, LH, LD, BX, BY, FIN, SWP,
    acc, GDS, GDR, gd_stage, lay_stage, gg_stage, gu_stage, send_sem, recv_sem, in_sem, out_sem,
):
    dp, t = lax.axis_index("dp"), lax.axis_index("tensor")
    x, yl = dp // 2, dp % 2
    yh, z, c = t // 8, (t // 2) % 4, t % 2
    x1, x0, z1, z0 = x // 2, x % 2, z // 2, z % 2

    def X(d):
        return (((x + d + 4) % 4) * 2 + yl, t)

    def Z(d):
        return (dp, yh * 8 + ((z + d + 4) % 4) * 2 + c)

    YL = (x * 2 + 1 - yl, t)
    YH = (dp, (1 - yh) * 8 + z * 2 + c)
    CORE = (dp, t + 1 - 2 * c)
    T1 = (dp, yh * 8 + (2 * z0 + (x0 + z1) % 2) * 2 + c)
    T1S = (dp, yh * 8 + (2 * ((x0 + z0) % 2) + z1) * 2 + c)
    hz = (x0 + z0) % 2
    t1_keep = T1[1] == t

    def owner(b):
        return ((2 * b + hz) * 2 + yl, t)

    def tok(dx):
        return (x + dx + 4) % 4

    def place(dz, b):
        at = (z + dz + 4) % 4
        return 2 * b + (x0 + at) % 2, at // 2

    barrier = pltpu.get_barrier_semaphore()
    greeted = (X(1), X(-1), YL, Z(1), Z(-1), YH, CORE, T1, T1S, owner(0), owner(1))
    for other in greeted:
        pl.semaphore_signal(barrier, inc=1, device_id=other, device_id_type=MESH)
    loads = []
    for n, (src, dst) in enumerate(((w_in, W2.at[yl]), (gate_in, gate), (up_in, up), (cot_in, cot))):
        loads.append(pltpu.make_async_copy(src, dst, in_sem.at[n]))
        loads[-1].start()

    def make_hidden(k, _):
        rows = pl.ds(pl.multiple_of(k * 32, 32), 32)
        g = gate[rows, :].astype(F32)
        HT[x, rows, :] = (g * jax.nn.sigmoid(g) * up[rows, :].astype(F32)).astype(BF)
        return 0

    loads[3].wait()
    for r in range(0, HALF, 128):
        OWN[:, r : r + 128] = cot[r : r + 128, :].astype(F32).T.astype(BF)
    loads[0].wait()
    loads[1].wait()
    loads[2].wait()
    lax.fori_loop(0, 29, make_hidden, 0)

    pl.semaphore_wait(barrier, len(greeted))
    cp = Copies(send_sem, recv_sem)
    low, high = pl.ds(0, CUT), pl.ds(CUT, FF - CUT)

    def crow(k, size=RC):
        return pl.ds(pl.multiple_of(c * HALF + k, 16), size)

    def share(ref, target):
        return cp.put(ref, ref, target)

    t1 = []
    for k in range(C):
        at = pl.ds(k * RC, RC)
        t1.append(cp.put_or_keep(t1_keep, OWN.at[at], ZM.at[0, at], T1)[1])

    def send_w(start, size):
        return share(W2.at[yl, :, pl.ds(start, size)], YL)

    ws = [send_w(0, 128)]
    a0, a1 = pl.ds(0, 240), pl.ds(FF - 240, 240)
    s1p, s1m = [share(HT.at[x, a0], X(1))], [share(HT.at[x, a1], X(-1))]

    def turn(s, n):
        WT[s, pl.ds(n * 256, 256), :] = W2[s, :, pl.ds(n * 256, 256)].astype(F32).T.astype(BF)

    t2_at = [cp.ids(2) for _ in range(C)]

    def send_t2(n, k):
        b = (n + yh) % 2
        at = pl.ds(k * RC, RC)
        cp.put_or_keep(
            2 * b + hz == x, ZM.at[n, at], CT.at[2 * x + z1, crow(k * RC)], owner(b), (t2_at[k] + n, t2_at[k] + x1)
        )

    def spread(b, k):
        token, s = place(0, b)
        ref = CT.at[2 * token + s, crow(k * RC)]
        return share(ref, Z(1)), share(ref, Z(-1))

    def forward(b, k):
        token, s = place(-1, b)
        lower = CT.at[2 * token + s, crow(k * RC, HC)]
        token, s = place(1, b)
        upper = CT.at[2 * token + s, crow(k * RC + HC, HC)]
        return share(lower, Z(1)), share(upper, Z(-1))

    t5, near, far = [], {}, {}

    def cross(dz, b):
        token, s = place(dz, b)
        t5.append(share(CT.at[2 * token + s, crow(0, HALF)], CORE))

    def owned(k):
        for b in range(2):
            landing = CT.at[2 * (2 * b + hz) + z1, crow(k * RC)]
            cp.landed(2 * b + hz == x, ZM.at[0, pl.ds(k * RC, RC)], landing, t2_at[k] + b, owner(b))
            near[b, k] = spread(b, k)

    t3 = []
    for k in range(C):
        at = pl.ds(k * RC, RC)
        cp.landed(t1_keep, OWN.at[at], ZM.at[0, at], t1[k], T1)
        t3.append(cp.put(ZM.at[0, at], ZM.at[1, at], YH))
        send_t2(0, k)
        if k > 0:
            t3[k - 1].wait_recv()
            send_t2(1, k - 1)
    owned(0)
    t3[-1].wait_recv()
    send_t2(1, C - 1)
    a0b, a1b = pl.ds(240, CUT - 240), pl.ds(CUT, FF - 240 - CUT)
    s1p.append(share(HT.at[x, a0b], X(1)))
    s1m.append(share(HT.at[x, a1b], X(-1)))
    for start, size in ((128, 128), (512, 256), (256, 256), (768, 256)):
        ws.append(send_w(start, size))
    s1p.append(share(HT.at[x, high], X(1)))
    s1m.append(share(HT.at[x, low], X(-1)))

    for k in range(1, C):
        owned(k)
    for n in range(4):
        turn(yl, n)

    def make_layer(s, k, first, step, count):
        def part(n, _):
            g, cols = (x + first + step * (n // 2)) % 4, pl.ds(pl.multiple_of((n % 2) * 256, 256), 256)
            there = pl.ds(pl.multiple_of((1 - c) * HALF + k * RL, RL), RL)
            here = pl.ds(pl.multiple_of(c * HALF + k * RL, RL), RL)
            h = HT[g, :, cols]
            LS[s, k, g, :, cols] = nn(WT[s, there, :], h).astype(BF)
            LO[s, k, g, :, cols] = nn(WT[s, here, :], h).astype(BF)
            return 0

        lax.fori_loop(0, 2 * count, part, 0)

    def cross_layer(s, k):
        return cp.put(LS.at[s, k], LX.at[s, k], CORE)

    cross(0, 0)
    cross(0, 1)
    s1p[0].wait_recv()
    s1m[0].wait_recv()
    s2 = [share(HT.at[tok(-1), a0], X(1)), share(HT.at[tok(1), a1], X(-1))]
    make_layer(yl, 0, 0, 1, 1)
    make_layer(yl, 1, 0, 1, 1)
    s1p[1].wait_recv()
    s1m[1].wait_recv()
    s2 += [share(HT.at[tok(-1), a0b], X(1)), share(HT.at[tok(1), a1b], X(-1))]

    for k in range(C):
        for b in range(2):
            near[b, k][0].wait_recv()
            near[b, k][1].wait_recv()
            far[b, k] = forward(b, k)
    for b in range(2):
        cross(1, b)
        cross(-1, b)
    s1p[2].wait_recv()
    s1m[2].wait_recv()
    make_layer(yl, 0, 1, 2, 2)
    make_layer(yl, 1, 1, 2, 2)
    for w in ws[:3]:
        w.wait_recv()
    turn(1 - yl, 0)
    turn(1 - yl, 2)
    make_layer(1 - yl, 0, 0, 1, 2)
    make_layer(1 - yl, 0, 3, 1, 1)
    for f in s2:
        f.wait_recv()
    make_layer(yl, 0, 2, 1, 1)
    lx = {0: cross_layer(yl, 0)}
    make_layer(1 - yl, 0, 2, 1, 1)
    lx[1] = cross_layer(1 - yl, 0)
    for b in range(2):
        for k in range(C):
            far[b, k][0].wait_recv()
            far[b, k][1].wait_recv()
        cross(2, b)

    def weight_sum(s, n):
        cols = pl.ds(n * 256, 256)
        acc[...] = jnp.zeros_like(acc)

        def add(g, _):
            acc[...] += nt(HT[g], CT[2 * g + s, cols, :])
            return 0

        lax.fori_loop(0, 4, add, 0)

    gd = {}

    def partner_sum(n):
        weight_sum(1 - yl, n)
        GDS[n] = acc[...].astype(BF)

    def send_sum(n, start=0, size=FF):
        at = pl.ds(start, size)
        gd.setdefault(n, []).append(cp.put(GDS.at[n, at], GDR.at[n, at], YL))

    def make_grad(g):
        def part(k, _):
            cols = pl.ds(pl.multiple_of(k * 256, 256), 256)
            G[g, :, cols] = (nn(W2[0], CT[2 * g, :, cols]) + nn(W2[1], CT[2 * g + 1, :, cols])).astype(BF)
            return 0

        lax.fori_loop(0, 2, part, 0)

    def pair(dz, b, k):
        token, s = place(dz, b)
        LO[s, k, token] = (LO[s, k, token].astype(F32) + LX[s, k, token].astype(F32)).astype(BF)

    halves, directs = {}, {}

    def begin(k):
        for b in range(2):
            pair(2, b, k)
            token, s = place(2, b)
            halves[b, k] = (
                cp.put(LO.at[s, k, token, pl.ds(0, HL)], LH.at[b, 0, k], Z(1)),
                cp.put(LO.at[s, k, token, pl.ds(HL, HL)], LH.at[b, 1, k], Z(-1)),
            )
        for b in range(2):
            pair(1, b, k)
            pair(-1, b, k)

    def relay(b, k):
        sent = []
        for side, dz in ((0, 1), (1, -1)):
            token, s = place(dz, b)
            halves[b, k][side].wait_recv()
            at = pl.ds(side * HL, HL)
            LO[s, k, token, at] = (LO[s, k, token, at].astype(F32) + LH[b, side, k].astype(F32)).astype(BF)
            sent.append(cp.put(LO.at[s, k, token], LD.at[b, side, k], Z(dz)))
        directs[b, k] = sent

    back_at = [cp.ids(2) for _ in range(CL)]

    def send_back(b, k):
        token, s = place(0, b)
        directs[b, k][0].wait_recv()
        directs[b, k][1].wait_recv()
        LO[s, k, token] = (
            LO[s, k, token].astype(F32) + LD[b, 0, k].astype(F32) + LD[b, 1, k].astype(F32)
        ).astype(BF)
        cp.put_or_keep(token == x, LO.at[s, k, token], BX.at[x1, k], owner(b), (back_at[k] + b, back_at[k] + x1))

    lx[0].wait_recv()
    lx[1].wait_recv()
    begin(0)
    for f in t5:
        f.wait_recv()
    partner_sum(0)
    send_sum(0)
    make_layer(yl, 1, 2, 1, 1)
    lx[2] = cross_layer(yl, 1)
    ws[3].wait_recv()
    ws[4].wait_recv()
    turn(1 - yl, 1)
    turn(1 - yl, 3)
    make_layer(1 - yl, 1, 0, 1, 4)
    lx[3] = cross_layer(1 - yl, 1)
    relay(0, 0)
    relay(1, 0)
    make_grad(tok(2))
    g2a = cp.put(G.at[tok(2), low], RAB.at[low], X(1))
    g2b = cp.put(G.at[tok(2), high], RAB.at[high], X(-1))
    partner_sum(1)
    send_sum(1)
    lx[2].wait_recv()
    lx[3].wait_recv()
    begin(1)
    for k in range(CL):
        pair(0, 0, k)
        pair(0, 1, k)
    up_one, down_one = tok(1), tok(-1)
    make_grad(up_one)
    partner_sum(2)
    send_sum(2)
    send_back(0, 0)
    send_back(1, 0)
    g5 = [cp.put(G.at[up_one, high], RO.at[0, high], X(1))]
    make_grad(down_one)
    g5.append(cp.put(G.at[down_one, low], RO.at[1, low], X(-1)))
    relay(0, 1)
    relay(1, 1)
    partner_sum(3)

    ly = []

    def meet(k):
        for r in range(2):
            cp.landed(2 * r + hz == x, LO.at[0, 0, 0], BX.at[r, k], back_at[k] + r, owner(r))
        ly.append(cp.put(BX.at[1 - yh, k], BY.at[k], YH))

    meet(0)
    send_sum(3, 0, CUT)
    g2a.wait_recv()
    G[up_one, low] = (G[up_one, low].astype(F32) + RAB[low].astype(F32)).astype(BF)
    g2b.wait_recv()
    G[down_one, high] = (G[down_one, high].astype(F32) + RAB[high].astype(F32)).astype(BF)
    send_back(0, 1)
    send_back(1, 1)
    g5.append(cp.put(G.at[up_one, low], RO.at[0, low], X(1)))
    g5.append(cp.put(G.at[down_one, high], RO.at[1, high], X(-1)))
    make_grad(x)

    sw = []

    def home(k):
        ly[k].wait_recv()
        at = pl.ds(k * RL, RL)
        FIN[at] = (BX[yh, k].astype(F32) + BY[k].astype(F32)).astype(BF)
        sw.append(cp.put_or_keep(t1_keep, FIN.at[at], SWP.at[at], T1S)[1])

    outs = []

    def own_sum(n):
        weight_sum(yl, n)
        for f in gd[n]:
            f.wait_recv()
        if n > 1:
            outs[n - 2].wait()
        gd_stage[n % 2] = (acc[...] + GDR[n].astype(F32)).astype(BF)
        copy = pltpu.make_async_copy(gd_stage.at[n % 2], gd_out.at[:, pl.ds(n * 256, 256)], out_sem.at[n])
        copy.start()
        outs.append(copy)

    own_sum(0)
    meet(1)
    send_sum(3, CUT, FF - CUT)
    home(0)
    own_sum(1)
    home(1)

    for f in g5:
        f.wait_recv()

    def finish(k, _):
        rows = pl.ds(pl.multiple_of(k * 32, 32), 32)
        total = G[x, rows, :].astype(F32) + RO[0, rows, :].astype(F32) + RO[1, rows, :].astype(F32)
        g = gate[rows, :].astype(F32)
        squash = jax.nn.sigmoid(g)
        gu_stage[rows, :] = (total * g * squash).astype(BF)
        gg_stage[rows, :] = (
            total * up[rows, :].astype(F32) * squash * (1.0 + g * (1.0 - squash))
        ).astype(BF)
        return 0

    lax.fori_loop(0, 29, finish, 0)
    for n, (stage, out) in enumerate(((gg_stage, gg_out), (gu_stage, gu_out))):
        copy = pltpu.make_async_copy(stage, out, out_sem.at[5 + n])
        copy.start()
        outs.append(copy)
    weight_sum(yl, 2)
    gd[2][0].wait_recv()
    outs[0].wait()
    gd_stage[0] = (acc[...] + GDR[2].astype(F32)).astype(BF)
    third = pltpu.make_async_copy(gd_stage.at[0], gd_out.at[:, pl.ds(512, 256)], out_sem.at[2])
    third.start()
    weight_sum(yl, 3)

    for k in range(CL):
        at = pl.ds(k * RL, RL)
        cp.landed(t1_keep, FIN.at[at], SWP.at[at], sw[k], T1S)
        for r in range(0, TOK, 128):
            lay_stage[r : r + 128, k * RL : (k + 1) * RL] = SWP[at, r : r + 128].astype(F32).T.astype(BF)
    lay = pltpu.make_async_copy(lay_stage, lay_out, out_sem.at[4])
    lay.start()
    cp.finish()
    outs[1].wait()
    gd[3][0].wait_recv()
    gd[3][1].wait_recv()
    gd_stage[1] = (acc[...] + GDR[3].astype(F32)).astype(BF)
    fourth = pltpu.make_async_copy(gd_stage.at[1], gd_out.at[:, pl.ds(768, 256)], out_sem.at[3])
    fourth.start()
    for copy in (outs[2], outs[3], third, lay, fourth):
        copy.wait()


def place_outputs(*refs):
    sources, results, stages, sems = refs[:4], refs[4:8], refs[8:12], refs[12]
    arrive, leave = [], []
    for n in (0, 3, 1, 2):
        rows = sources[n].shape[0] // 2
        for part in range(2):
            at, k = pl.ds(part * rows, rows), len(arrive)
            arrive.append(pltpu.make_async_copy(sources[n].at[at], stages[n].at[at], sems.at[k]))
            leave.append(pltpu.make_async_copy(stages[n].at[at], results[n].at[at], sems.at[8 + k]))
    for copy in arrive:
        copy.start()
    for k in range(8):
        arrive[k].wait()
        leave[k].start()
    for copy in leave:
        copy.wait()


def shards(gate_pre, up_pre, w_down, cotangent):
    anywhere = pl.BlockSpec(memory_space=pl.ANY)
    n_copies = 140
    flops = 2 * 3 * TOK * FF * 8192
    shapes = (
        jax.ShapeDtypeStruct((TOK, HALF), BF),
        jax.ShapeDtypeStruct((FF, TOK), BF),
        jax.ShapeDtypeStruct((FF, TOK), BF),
        jax.ShapeDtypeStruct((FF, DM), BF),
    )
    results = pl.pallas_call(
        kernel,
        out_shape=shapes,
        in_specs=[anywhere] * 4,
        out_specs=[anywhere] * 4,
        scratch_shapes=[
            pltpu.VMEM((FF, TOK), BF),
            pltpu.VMEM((FF, TOK), BF),
            pltpu.VMEM((TOK, HALF), BF),
            pltpu.VMEM((2, FF, DM), BF),
            pltpu.VMEM((2, DM, FF), BF),
            pltpu.VMEM((4, FF, TOK), BF),
            pltpu.VMEM((8, DM, TOK), BF),
            pltpu.VMEM((HALF, TOK), BF),
            pltpu.VMEM((2, HALF, TOK), BF),
            pltpu.VMEM((4, FF, TOK), BF),
            pltpu.VMEM((FF, TOK), BF),
            pltpu.VMEM((2, FF, TOK), BF),
            pltpu.VMEM((2, CL, 4, RL, TOK), BF),
            pltpu.VMEM((2, CL, 4, RL, TOK), BF),
            pltpu.VMEM((2, CL, 4, RL, TOK), BF),
            pltpu.VMEM((2, 2, CL, HL, TOK), BF),
            pltpu.VMEM((2, 2, CL, RL, TOK), BF),
            pltpu.VMEM((2, CL, RL, TOK), BF),
            pltpu.VMEM((CL, RL, TOK), BF),
            pltpu.VMEM((HALF, TOK), BF),
            pltpu.VMEM((HALF, TOK), BF),
            pltpu.VMEM((FF, 256), F32),
            pltpu.VMEM((4, FF, 256), BF),
            pltpu.VMEM((4, FF, 256), BF),
            pltpu.VMEM((2, FF, 256), BF),
            pltpu.VMEM((TOK, HALF), BF),
            pltpu.VMEM((FF, TOK), BF),
            pltpu.VMEM((FF, TOK), BF),
            pltpu.SemaphoreType.DMA((n_copies,)),
            pltpu.SemaphoreType.DMA((n_copies,)),
            pltpu.SemaphoreType.DMA((4,)),
            pltpu.SemaphoreType.DMA((7,)),
        ],
        compiler_params=pltpu.CompilerParams(
            collective_id=0, has_side_effects=True, vmem_limit_bytes=64 * 2**20
        ),
        cost_estimate=pl.CostEstimate(flops=flops, bytes_accessed=2**24, transcendentals=0),
    )(gate_pre.T, up_pre.T, w_down, cotangent)
    layer_out, grad_gate, grad_up, grad_down = pl.pallas_call(
        place_outputs,
        out_shape=shapes,
        in_specs=[anywhere] * 4,
        out_specs=[anywhere] * 4,
        scratch_shapes=[pltpu.VMEM(shape.shape, BF) for shape in shapes] + [pltpu.SemaphoreType.DMA((16,))],
        compiler_params=pltpu.CompilerParams(vmem_limit_bytes=64 * 2**20),
    )(*results)
    return layer_out, grad_gate.T, grad_up.T, grad_down


def solution(mesh):
    placed = (P("dp", "tensor"), P("dp", "tensor"), P("tensor", "dp"), P("dp", "tensor"))
    return jax.shard_map(
        shards,
        mesh=mesh,
        in_specs=placed,
        out_specs=(P("dp", "tensor"), P("dp", "tensor"), P("dp", "tensor"), P("tensor", "dp")),
        check_vma=False,
    )
```

```python
import jax
import jax.numpy as jnp
from jax import lax
from jax.experimental import pallas as pl
from jax.experimental.pallas import tpu as pltpu
from jax.sharding import PartitionSpec as P

MESH = pl.DeviceIdType.MESH
BF = jnp.bfloat16
F32 = jnp.float32

TOK = 512
FF = 928
DM = 1024
HALF = 512
CUT = 464
C = 4
RC = HALF // C
HC = RC // 2
CL = 2
RL = HALF // CL
HL = RL // 2


class Copies:
    def __init__(self, send, recv):
        self.send, self.recv, self.all, self.n = send, recv, [], 0

    def ids(self, count):
        self.n += count
        return self.n - count

    def put(self, src, dst, target):
        k = self.ids(1)
        copy = pltpu.make_async_remote_copy(
            src, dst, self.send.at[k], self.recv.at[k], device_id=target, device_id_type=MESH
        )
        copy.start()
        self.all.append((None, copy))
        return copy

    def put_or_keep(self, keep, src, dst, target, at=None):
        ks, kr = at or (self.ids(1),) * 2
        copy = pltpu.make_async_remote_copy(
            src, dst, self.send.at[ks], self.recv.at[kr], device_id=target, device_id_type=MESH
        )
        pl.when(keep)(pltpu.make_async_copy(src, dst, self.recv.at[kr]).start)
        pl.when(jnp.logical_not(keep))(copy.start)
        self.all.append((keep, copy))
        return ks, kr

    def landed(self, keep, src, landing, kr, target):
        got = pltpu.make_async_remote_copy(
            src, landing, self.send.at[kr], self.recv.at[kr], device_id=target, device_id_type=MESH
        )
        pl.when(keep)(pltpu.make_async_copy(src, landing, self.recv.at[kr]).wait)
        pl.when(jnp.logical_not(keep))(got.wait_recv)

    def finish(self):
        for keep, copy in self.all:
            if keep is None:
                copy.wait_send()
            else:
                pl.when(jnp.logical_not(keep))(copy.wait_send)
        self.all = []


def nn(a, b):
    return lax.dot_general(a, b, (((1,), (0,)), ((), ())), preferred_element_type=F32)


def nt(a, b):
    return lax.dot_general(a, b, (((1,), (1,)), ((), ())), preferred_element_type=F32)


def kernel(
    gate_in, up_in, w_in, cot_in, lay_out, gg_out, gu_out, gd_out,
    gate, up, cot, W2, WT, HT, CT, OWN, ZM, G, RAB, RO, LO, LS, LX, LH, LD, BX, BY, FIN, SWP,
    acc, GDS, GDR, gd_stage, lay_stage, gg_stage, gu_stage, send_sem, recv_sem, in_sem, out_sem,
):
    dp, t = lax.axis_index("dp"), lax.axis_index("tensor")
    x, yl = dp // 2, dp % 2
    yh, z, c = t // 8, (t // 2) % 4, t % 2
    x1, x0, z1, z0 = x // 2, x % 2, z // 2, z % 2

    def X(d):
        return (((x + d + 4) % 4) * 2 + yl, t)

    def Z(d):
        return (dp, yh * 8 + ((z + d + 4) % 4) * 2 + c)

    YL = (x * 2 + 1 - yl, t)
    YH = (dp, (1 - yh) * 8 + z * 2 + c)
    CORE = (dp, t + 1 - 2 * c)
    T1 = (dp, yh * 8 + (2 * z0 + (x0 + z1) % 2) * 2 + c)
    T1S = (dp, yh * 8 + (2 * ((x0 + z0) % 2) + z1) * 2 + c)
    hz = (x0 + z0) % 2
    t1_keep = T1[1] == t

    def owner(b):
        return ((2 * b + hz) * 2 + yl, t)

    def tok(dx):
        return (x + dx + 4) % 4

    def place(dz, b):
        at = (z + dz + 4) % 4
        return 2 * b + (x0 + at) % 2, at // 2

    barrier = pltpu.get_barrier_semaphore()
    greeted = (X(1), X(-1), YL, Z(1), Z(-1), YH, CORE, T1, T1S, owner(0), owner(1))
    for other in greeted:
        pl.semaphore_signal(barrier, inc=1, device_id=other, device_id_type=MESH)
    loads = []
    for n, (src, dst) in enumerate(((cot_in, cot), (gate_in, gate), (up_in, up), (w_in, W2.at[yl]))):
        loads.append(pltpu.make_async_copy(src, dst, in_sem.at[n]))
        loads[-1].start()

    def make_hidden(k, _):
        rows = pl.ds(pl.multiple_of(k * 32, 32), 32)
        g = gate[rows, :].astype(F32)
        HT[x, rows, :] = (g * jax.nn.sigmoid(g) * up[rows, :].astype(F32)).astype(BF)
        return 0

    loads[0].wait()
    for r in range(0, HALF, 128):
        OWN[:, r : r + 128] = cot[r : r + 128, :].astype(F32).T.astype(BF)

    pl.semaphore_wait(barrier, len(greeted))
    cp = Copies(send_sem, recv_sem)
    low, high = pl.ds(0, CUT), pl.ds(CUT, FF - CUT)

    def crow(k, size=RC):
        return pl.ds(pl.multiple_of(c * HALF + k, 16), size)

    def share(ref, target):
        return cp.put(ref, ref, target)

    t1 = []
    for k in range(C):
        at = pl.ds(k * RC, RC)
        t1.append(cp.put_or_keep(t1_keep, OWN.at[at], ZM.at[0, at], T1)[1])

    loads[1].wait()
    loads[2].wait()
    lax.fori_loop(0, 29, make_hidden, 0)
    a0, a1 = pl.ds(0, 240), pl.ds(FF - 240, 240)
    s1p, s1m = [share(HT.at[x, a0], X(1))], [share(HT.at[x, a1], X(-1))]
    loads[3].wait()

    def send_w(start, size):
        return share(W2.at[yl, :, pl.ds(start, size)], YL)

    ws = [send_w(0, 128)]

    def turn(s, n):
        WT[s, pl.ds(n * 256, 256), :] = W2[s, :, pl.ds(n * 256, 256)].astype(F32).T.astype(BF)

    t2_at = [cp.ids(2) for _ in range(C)]

    def send_t2(n, k):
        b = (n + yh) % 2
        at = pl.ds(k * RC, RC)
        cp.put_or_keep(
            2 * b + hz == x, ZM.at[n, at], CT.at[2 * x + z1, crow(k * RC)], owner(b), (t2_at[k] + n, t2_at[k] + x1)
        )

    def spread(b, k):
        token, s = place(0, b)
        ref = CT.at[2 * token + s, crow(k * RC)]
        return share(ref, Z(1)), share(ref, Z(-1))

    def forward(b, k):
        token, s = place(-1, b)
        lower = CT.at[2 * token + s, crow(k * RC, HC)]
        token, s = place(1, b)
        upper = CT.at[2 * token + s, crow(k * RC + HC, HC)]
        return share(lower, Z(1)), share(upper, Z(-1))

    t5, near, far = [], {}, {}

    def cross(dz, b):
        token, s = place(dz, b)
        t5.append(share(CT.at[2 * token + s, crow(0, HALF)], CORE))

    def owned(k):
        for b in range(2):
            landing = CT.at[2 * (2 * b + hz) + z1, crow(k * RC)]
            cp.landed(2 * b + hz == x, ZM.at[0, pl.ds(k * RC, RC)], landing, t2_at[k] + b, owner(b))
            near[b, k] = spread(b, k)

    t3 = []
    for k in range(C):
        at = pl.ds(k * RC, RC)
        cp.landed(t1_keep, OWN.at[at], ZM.at[0, at], t1[k], T1)
        t3.append(cp.put(ZM.at[0, at], ZM.at[1, at], YH))
        send_t2(0, k)
        if k > 0:
            t3[k - 1].wait_recv()
            send_t2(1, k - 1)
    owned(0)
    t3[-1].wait_recv()
    send_t2(1, C - 1)
    a0b, a1b = pl.ds(240, CUT - 240), pl.ds(CUT, FF - 240 - CUT)
    s1p.append(share(HT.at[x, a0b], X(1)))
    s1m.append(share(HT.at[x, a1b], X(-1)))
    for start, size in ((128, 128), (512, 256), (256, 256), (768, 256)):
        ws.append(send_w(start, size))
    s1p.append(share(HT.at[x, high], X(1)))
    s1m.append(share(HT.at[x, low], X(-1)))

    for k in range(1, C):
        owned(k)
    for n in range(4):
        turn(yl, n)

    lx = {}

    def make_layer(other, k, first, step, count):
        s = 1 - yl if other else yl

        def part(n, _):
            g, cols = (x + first + step * (n // 2)) % 4, pl.ds(pl.multiple_of((n % 2) * 256, 256), 256)
            there = pl.ds(pl.multiple_of((1 - c) * HALF + k * RL, RL), RL)
            here = pl.ds(pl.multiple_of(c * HALF + k * RL, RL), RL)
            h = HT[g, :, cols]
            LS[s, k, g, :, cols] = nn(WT[s, there, :], h).astype(BF)
            LO[s, k, g, :, cols] = nn(WT[s, here, :], h).astype(BF)
            return 0

        lax.fori_loop(0, 2 * count, part, 0)

        for n in range(count):
            g = (x + first + step * n) % 4
            lx.setdefault((other, k), []).append(cp.put(LS.at[s, k, g], LX.at[s, k, g], CORE))

    cross(0, 0)
    cross(0, 1)
    s1p[0].wait_recv()
    s1m[0].wait_recv()
    s2 = [share(HT.at[tok(-1), a0], X(1)), share(HT.at[tok(1), a1], X(-1))]
    make_layer(False, 0, 0, 1, 1)
    make_layer(False, 1, 0, 1, 1)
    s1p[1].wait_recv()
    s1m[1].wait_recv()
    s2 += [share(HT.at[tok(-1), a0b], X(1)), share(HT.at[tok(1), a1b], X(-1))]

    for k in range(C):
        for b in range(2):
            near[b, k][0].wait_recv()
            near[b, k][1].wait_recv()
            far[b, k] = forward(b, k)
        if k == 1:
            s1p[2].wait_recv()
            s1m[2].wait_recv()
            make_layer(False, 0, 1, 2, 2)
        if k == 2:
            make_layer(False, 1, 1, 2, 2)
            ws[0].wait_recv()
            ws[1].wait_recv()
            turn(1 - yl, 0)
    for b in range(2):
        cross(1, b)
        cross(-1, b)
    ws[2].wait_recv()
    turn(1 - yl, 2)
    make_layer(True, 0, 0, 1, 2)
    make_layer(True, 0, 3, 1, 1)
    for f in s2:
        f.wait_recv()
    make_layer(False, 0, 2, 1, 1)
    make_layer(True, 0, 2, 1, 1)
    for b in range(2):
        for k in range(C):
            far[b, k][0].wait_recv()
            far[b, k][1].wait_recv()
        cross(2, b)

    def weight_sum(s, n):
        cols = pl.ds(n * 256, 256)
        acc[...] = jnp.zeros_like(acc)

        def add(g, _):
            acc[...] += nt(HT[g], CT[2 * g + s, cols, :])
            return 0

        lax.fori_loop(0, 4, add, 0)

    gd = {}

    def partner_sum(n):
        weight_sum(1 - yl, n)
        GDS[n] = acc[...].astype(BF)

    def send_sum(n, start=0, size=FF):
        at = pl.ds(start, size)
        gd.setdefault(n, []).append(cp.put(GDS.at[n, at], GDR.at[n, at], YL))

    def make_grad(g):
        def part(k, _):
            cols = pl.ds(pl.multiple_of(k * 256, 256), 256)
            G[g, :, cols] = (nn(W2[0], CT[2 * g, :, cols]) + nn(W2[1], CT[2 * g + 1, :, cols])).astype(BF)
            return 0

        lax.fori_loop(0, 2, part, 0)

    def pair(dz, b, k):
        token, s = place(dz, b)
        LO[s, k, token] = (LO[s, k, token].astype(F32) + LX[s, k, token].astype(F32)).astype(BF)

    halves, directs = {}, {}

    def begin(k):
        for b in range(2):
            pair(2, b, k)
            token, s = place(2, b)
            halves[b, k] = (
                cp.put(LO.at[s, k, token, pl.ds(0, HL)], LH.at[b, 0, k], Z(1)),
                cp.put(LO.at[s, k, token, pl.ds(HL, HL)], LH.at[b, 1, k], Z(-1)),
            )
        for b in range(2):
            pair(1, b, k)
            pair(-1, b, k)

    def relay(b, k):
        sent = []
        for side, dz in ((0, 1), (1, -1)):
            token, s = place(dz, b)
            halves[b, k][side].wait_recv()
            at = pl.ds(side * HL, HL)
            LO[s, k, token, at] = (LO[s, k, token, at].astype(F32) + LH[b, side, k].astype(F32)).astype(BF)
            sent.append(cp.put(LO.at[s, k, token], LD.at[b, side, k], Z(dz)))
        directs[b, k] = sent

    back_at = [cp.ids(2) for _ in range(CL)]

    def send_back(b, k):
        token, s = place(0, b)
        directs[b, k][0].wait_recv()
        directs[b, k][1].wait_recv()
        LO[s, k, token] = (
            LO[s, k, token].astype(F32) + LD[b, 0, k].astype(F32) + LD[b, 1, k].astype(F32)
        ).astype(BF)
        cp.put_or_keep(token == x, LO.at[s, k, token], BX.at[x1, k], owner(b), (back_at[k] + b, back_at[k] + x1))

    for other in range(2):
        for f in lx[other, 0]:
            f.wait_recv()
    begin(0)
    for f in t5:
        f.wait_recv()
    partner_sum(0)
    send_sum(0)
    make_layer(False, 1, 2, 1, 1)
    ws[3].wait_recv()
    ws[4].wait_recv()
    make_grad(tok(2))
    g2a = cp.put(G.at[tok(2), low], RAB.at[low], X(1))
    g2b = cp.put(G.at[tok(2), high], RAB.at[high], X(-1))
    relay(0, 0)
    turn(1 - yl, 1)
    turn(1 - yl, 3)
    make_layer(True, 1, 0, 1, 2)
    relay(1, 0)
    make_layer(True, 1, 2, 1, 2)
    partner_sum(1)
    send_sum(1)
    for other in range(2):
        for f in lx[other, 1]:
            f.wait_recv()
    begin(1)
    for k in range(CL):
        pair(0, 0, k)
        pair(0, 1, k)
    up_one, down_one = tok(1), tok(-1)
    make_grad(up_one)
    send_back(0, 0)
    g5 = [cp.put(G.at[up_one, high], RO.at[0, high], X(1))]
    partner_sum(2)
    send_sum(2)
    send_back(1, 0)
    make_grad(down_one)
    g5.append(cp.put(G.at[down_one, low], RO.at[1, low], X(-1)))
    relay(0, 1)
    relay(1, 1)
    partner_sum(3)

    ly = []

    def meet(k):
        for r in range(2):
            cp.landed(2 * r + hz == x, LO.at[0, 0, 0], BX.at[r, k], back_at[k] + r, owner(r))
        ly.append(cp.put(BX.at[1 - yh, k], BY.at[k], YH))

    meet(0)
    send_sum(3, 0, CUT)
    g2a.wait_recv()
    G[up_one, low] = (G[up_one, low].astype(F32) + RAB[low].astype(F32)).astype(BF)
    g2b.wait_recv()
    G[down_one, high] = (G[down_one, high].astype(F32) + RAB[high].astype(F32)).astype(BF)
    send_back(0, 1)
    send_back(1, 1)
    g5.append(cp.put(G.at[up_one, low], RO.at[0, low], X(1)))
    g5.append(cp.put(G.at[down_one, high], RO.at[1, high], X(-1)))
    make_grad(x)

    sw = []

    def home(k):
        ly[k].wait_recv()
        at = pl.ds(k * RL, RL)
        FIN[at] = (BX[yh, k].astype(F32) + BY[k].astype(F32)).astype(BF)
        sw.append(cp.put_or_keep(t1_keep, FIN.at[at], SWP.at[at], T1S)[1])

    outs = []

    def own_sum(n):
        weight_sum(yl, n)
        for f in gd[n]:
            f.wait_recv()
        if n > 1:
            outs[n - 2].wait()
        gd_stage[n % 2] = (acc[...] + GDR[n].astype(F32)).astype(BF)
        copy = pltpu.make_async_copy(gd_stage.at[n % 2], gd_out.at[:, pl.ds(n * 256, 256)], out_sem.at[n])
        copy.start()
        outs.append(copy)

    own_sum(0)
    meet(1)
    send_sum(3, CUT, FF - CUT)
    home(0)
    own_sum(1)
    weight_sum(yl, 2)
    gd[2][0].wait_recv()
    outs[0].wait()
    gd_stage[0] = (acc[...] + GDR[2].astype(F32)).astype(BF)
    third = pltpu.make_async_copy(gd_stage.at[0], gd_out.at[:, pl.ds(512, 256)], out_sem.at[2])
    third.start()
    weight_sum(yl, 3)
    home(1)

    for f in g5:
        f.wait_recv()

    def finish(k, _):
        rows = pl.ds(pl.multiple_of(k * 32, 32), 32)
        total = G[x, rows, :].astype(F32) + RO[0, rows, :].astype(F32) + RO[1, rows, :].astype(F32)
        g = gate[rows, :].astype(F32)
        squash = jax.nn.sigmoid(g)
        gu_stage[rows, :] = (total * g * squash).astype(BF)
        gg_stage[rows, :] = (
            total * up[rows, :].astype(F32) * squash * (1.0 + g * (1.0 - squash))
        ).astype(BF)
        return 0

    lax.fori_loop(0, 29, finish, 0)
    for n, (stage, out) in enumerate(((gg_stage, gg_out), (gu_stage, gu_out))):
        copy = pltpu.make_async_copy(stage, out, out_sem.at[5 + n])
        copy.start()
        outs.append(copy)
    gd[3][0].wait_recv()
    gd[3][1].wait_recv()
    outs[1].wait()
    gd_stage[1] = (acc[...] + GDR[3].astype(F32)).astype(BF)
    fourth = pltpu.make_async_copy(gd_stage.at[1], gd_out.at[:, pl.ds(768, 256)], out_sem.at[3])
    fourth.start()
    cp.finish()

    for k in range(CL):
        at = pl.ds(k * RL, RL)
        cp.landed(t1_keep, FIN.at[at], SWP.at[at], sw[k], T1S)
        for r in range(0, TOK, 128):
            lay_stage[r : r + 128, k * RL : (k + 1) * RL] = SWP[at, r : r + 128].astype(F32).T.astype(BF)
    lay = pltpu.make_async_copy(lay_stage, lay_out, out_sem.at[4])
    lay.start()
    cp.finish()
    for copy in (outs[2], outs[3], third, lay, fourth):
        copy.wait()


def place_outputs(*refs):
    sources, results, stages, sems = refs[:4], refs[4:8], refs[8:12], refs[12]
    arrive, leave = [], []
    for n in (0, 3, 1, 2):
        rows = sources[n].shape[0] // 2
        for part in range(2):
            at, k = pl.ds(part * rows, rows), len(arrive)
            arrive.append(pltpu.make_async_copy(sources[n].at[at], stages[n].at[at], sems.at[k]))
            leave.append(pltpu.make_async_copy(stages[n].at[at], results[n].at[at], sems.at[8 + k]))
    for copy in arrive:
        copy.start()
    for k in range(8):
        arrive[k].wait()
        leave[k].start()
    for copy in leave:
        copy.wait()


def shards(gate_pre, up_pre, w_down, cotangent):
    anywhere = pl.BlockSpec(memory_space=pl.ANY)
    n_copies = 140
    flops = 2 * 3 * TOK * FF * 8192
    shapes = (
        jax.ShapeDtypeStruct((TOK, HALF), BF),
        jax.ShapeDtypeStruct((FF, TOK), BF),
        jax.ShapeDtypeStruct((FF, TOK), BF),
        jax.ShapeDtypeStruct((FF, DM), BF),
    )
    results = pl.pallas_call(
        kernel,
        out_shape=shapes,
        in_specs=[anywhere] * 4,
        out_specs=[anywhere] * 4,
        scratch_shapes=[
            pltpu.VMEM((FF, TOK), BF),
            pltpu.VMEM((FF, TOK), BF),
            pltpu.VMEM((TOK, HALF), BF),
            pltpu.VMEM((2, FF, DM), BF),
            pltpu.VMEM((2, DM, FF), BF),
            pltpu.VMEM((4, FF, TOK), BF),
            pltpu.VMEM((8, DM, TOK), BF),
            pltpu.VMEM((HALF, TOK), BF),
            pltpu.VMEM((2, HALF, TOK), BF),
            pltpu.VMEM((4, FF, TOK), BF),
            pltpu.VMEM((FF, TOK), BF),
            pltpu.VMEM((2, FF, TOK), BF),
            pltpu.VMEM((2, CL, 4, RL, TOK), BF),
            pltpu.VMEM((2, CL, 4, RL, TOK), BF),
            pltpu.VMEM((2, CL, 4, RL, TOK), BF),
            pltpu.VMEM((2, 2, CL, HL, TOK), BF),
            pltpu.VMEM((2, 2, CL, RL, TOK), BF),
            pltpu.VMEM((2, CL, RL, TOK), BF),
            pltpu.VMEM((CL, RL, TOK), BF),
            pltpu.VMEM((HALF, TOK), BF),
            pltpu.VMEM((HALF, TOK), BF),
            pltpu.VMEM((FF, 256), F32),
            pltpu.VMEM((4, FF, 256), BF),
            pltpu.VMEM((4, FF, 256), BF),
            pltpu.VMEM((2, FF, 256), BF),
            pltpu.VMEM((TOK, HALF), BF),
            pltpu.VMEM((FF, TOK), BF),
            pltpu.VMEM((FF, TOK), BF),
            pltpu.SemaphoreType.DMA((n_copies,)),
            pltpu.SemaphoreType.DMA((n_copies,)),
            pltpu.SemaphoreType.DMA((4,)),
            pltpu.SemaphoreType.DMA((7,)),
        ],
        compiler_params=pltpu.CompilerParams(
            collective_id=0, has_side_effects=True, vmem_limit_bytes=64 * 2**20
        ),
        cost_estimate=pl.CostEstimate(flops=flops, bytes_accessed=2**24, transcendentals=0),
    )(gate_pre.T, up_pre.T, w_down, cotangent)
    layer_out, grad_gate, grad_up, grad_down = pl.pallas_call(
        place_outputs,
        out_shape=shapes,
        in_specs=[anywhere] * 4,
        out_specs=[anywhere] * 4,
        scratch_shapes=[pltpu.VMEM(shape.shape, BF) for shape in shapes] + [pltpu.SemaphoreType.DMA((16,))],
        compiler_params=pltpu.CompilerParams(vmem_limit_bytes=64 * 2**20),
    )(*results)
    return layer_out, grad_gate.T, grad_up.T, grad_down


def solution(mesh):
    placed = (P("dp", "tensor"), P("dp", "tensor"), P("tensor", "dp"), P("dp", "tensor"))
    return jax.shard_map(
        shards,
        mesh=mesh,
        in_specs=placed,
        out_specs=(P("dp", "tensor"), P("dp", "tensor"), P("dp", "tensor"), P("tensor", "dp")),
        check_vma=False,
    )
```

```python
import jax
import jax.numpy as jnp
from jax import lax
from jax.experimental import pallas as pl
from jax.experimental.pallas import tpu as pltpu
from jax.sharding import PartitionSpec as P

MESH = pl.DeviceIdType.MESH
BF = jnp.bfloat16
F32 = jnp.float32

TOK = 512
FF = 928
DM = 1024
HALF = 512
CUT = 464
C = 4
RC = HALF // C
HC = RC // 2
CL = 2
RL = HALF // CL
HL = RL // 2


class Copies:
    def __init__(self, send, recv):
        self.send, self.recv, self.all, self.n = send, recv, [], 0

    def ids(self, count):
        self.n += count
        return self.n - count

    def put(self, src, dst, target):
        k = self.ids(1)
        copy = pltpu.make_async_remote_copy(
            src, dst, self.send.at[k], self.recv.at[k], device_id=target, device_id_type=MESH
        )
        copy.start()
        self.all.append((None, copy))
        return copy

    def put_or_keep(self, keep, src, dst, target, at=None):
        ks, kr = at or (self.ids(1),) * 2
        copy = pltpu.make_async_remote_copy(
            src, dst, self.send.at[ks], self.recv.at[kr], device_id=target, device_id_type=MESH
        )
        pl.when(keep)(pltpu.make_async_copy(src, dst, self.recv.at[kr]).start)
        pl.when(jnp.logical_not(keep))(copy.start)
        self.all.append((keep, copy))
        return ks, kr

    def landed(self, keep, src, landing, kr, target):
        got = pltpu.make_async_remote_copy(
            src, landing, self.send.at[kr], self.recv.at[kr], device_id=target, device_id_type=MESH
        )
        pl.when(keep)(pltpu.make_async_copy(src, landing, self.recv.at[kr]).wait)
        pl.when(jnp.logical_not(keep))(got.wait_recv)

    def finish(self):
        for keep, copy in self.all:
            if keep is None:
                copy.wait_send()
            else:
                pl.when(jnp.logical_not(keep))(copy.wait_send)
        self.all = []


def nn(a, b):
    return lax.dot_general(a, b, (((1,), (0,)), ((), ())), preferred_element_type=F32)


def nt(a, b):
    return lax.dot_general(a, b, (((1,), (1,)), ((), ())), preferred_element_type=F32)


def kernel(
    gate_in, up_in, w_in, cot_in, lay_out, gg_out, gu_out, gd_out,
    gate, up, cot, W2, WT, HT, CT, OWN, ZM, G, RAB, RO, LO, LS, LX, LH, LD, BX, BY, FIN, SWP,
    acc, GDS, GDR, gd_stage, lay_stage, gg_stage, gu_stage, send_sem, recv_sem, in_sem, out_sem,
):
    dp, t = lax.axis_index("dp"), lax.axis_index("tensor")
    x, yl = dp // 2, dp % 2
    yh, z, c = t // 8, (t // 2) % 4, t % 2
    x1, x0, z1, z0 = x // 2, x % 2, z // 2, z % 2

    def X(d):
        return (((x + d + 4) % 4) * 2 + yl, t)

    def Z(d):
        return (dp, yh * 8 + ((z + d + 4) % 4) * 2 + c)

    YL = (x * 2 + 1 - yl, t)
    YH = (dp, (1 - yh) * 8 + z * 2 + c)
    CORE = (dp, t + 1 - 2 * c)
    T1 = (dp, yh * 8 + (2 * z0 + (x0 + z1) % 2) * 2 + c)
    T1S = (dp, yh * 8 + (2 * ((x0 + z0) % 2) + z1) * 2 + c)
    hz = (x0 + z0) % 2
    t1_keep = T1[1] == t

    def owner(b):
        return ((2 * b + hz) * 2 + yl, t)

    def tok(dx):
        return (x + dx + 4) % 4

    def place(dz, b):
        at = (z + dz + 4) % 4
        return 2 * b + (x0 + at) % 2, at // 2

    barrier = pltpu.get_barrier_semaphore()
    greeted = (X(1), X(-1), YL, Z(1), Z(-1), YH, CORE, T1, T1S, owner(0), owner(1))
    for other in greeted:
        pl.semaphore_signal(barrier, inc=1, device_id=other, device_id_type=MESH)
    loads = []
    for n, (src, dst) in enumerate(((cot_in, cot), (gate_in, gate), (up_in, up), (w_in, W2.at[yl]))):
        loads.append(pltpu.make_async_copy(src, dst, in_sem.at[n]))
        loads[-1].start()

    def make_hidden(k, _):
        rows = pl.ds(pl.multiple_of(k * 32, 32), 32)
        g = gate[rows, :].astype(F32)
        HT[x, rows, :] = (g * jax.nn.sigmoid(g) * up[rows, :].astype(F32)).astype(BF)
        return 0

    loads[0].wait()
    for r in range(0, HALF, 128):
        OWN[:, r : r + 128] = cot[r : r + 128, :].astype(F32).T.astype(BF)

    pl.semaphore_wait(barrier, len(greeted))
    cp = Copies(send_sem, recv_sem)
    low, high = pl.ds(0, CUT), pl.ds(CUT, FF - CUT)

    def crow(k, size=RC):
        return pl.ds(pl.multiple_of(c * HALF + k, 16), size)

    def share(ref, target):
        return cp.put(ref, ref, target)

    t1 = []
    for k in range(C):
        at = pl.ds(k * RC, RC)
        t1.append(cp.put_or_keep(t1_keep, OWN.at[at], ZM.at[0, at], T1)[1])

    loads[1].wait()
    loads[2].wait()
    lax.fori_loop(0, 29, make_hidden, 0)
    a0, a1 = pl.ds(0, 240), pl.ds(FF - 240, 240)
    a0b, a1b = pl.ds(240, CUT - 240), pl.ds(CUT, FF - 240 - CUT)
    s1p, s1m = [share(HT.at[x, a0], X(1))], [share(HT.at[x, a1], X(-1))]
    loads[3].wait()

    def send_w(start, size):
        return share(W2.at[yl, :, pl.ds(start, size)], YL)

    ws = [send_w(0, 128)]

    def turn(s, n):
        WT[s, pl.ds(n * 256, 256), :] = W2[s, :, pl.ds(n * 256, 256)].astype(F32).T.astype(BF)

    t2_at = [cp.ids(2) for _ in range(C)]

    def send_t2(n, k):
        b = (n + yh) % 2
        at = pl.ds(k * RC, RC)
        cp.put_or_keep(
            2 * b + hz == x, ZM.at[n, at], CT.at[2 * x + z1, crow(k * RC)], owner(b), (t2_at[k] + n, t2_at[k] + x1)
        )

    def spread(b, k):
        token, s = place(0, b)
        ref = CT.at[2 * token + s, crow(k * RC)]
        return share(ref, Z(1)), share(ref, Z(-1))

    def forward(b, k):
        token, s = place(-1, b)
        lower = CT.at[2 * token + s, crow(k * RC, HC)]
        token, s = place(1, b)
        upper = CT.at[2 * token + s, crow(k * RC + HC, HC)]
        return share(lower, Z(1)), share(upper, Z(-1))

    t5, near, far = [], {}, {}

    def cross(dz, b):
        token, s = place(dz, b)
        t5.append(share(CT.at[2 * token + s, crow(0, HALF)], CORE))

    def owned(k):
        for b in range(2):
            landing = CT.at[2 * (2 * b + hz) + z1, crow(k * RC)]
            cp.landed(2 * b + hz == x, ZM.at[0, pl.ds(k * RC, RC)], landing, t2_at[k] + b, owner(b))
            near[b, k] = spread(b, k)

    t3 = []
    for k in range(C):
        at = pl.ds(k * RC, RC)
        cp.landed(t1_keep, OWN.at[at], ZM.at[0, at], t1[k], T1)
        t3.append(cp.put(ZM.at[0, at], ZM.at[1, at], YH))
        send_t2(0, k)
        if k > 0:
            t3[k - 1].wait_recv()
            send_t2(1, k - 1)
        if k == 1:
            s1p.append(share(HT.at[x, a0b], X(1)))
            s1m.append(share(HT.at[x, a1b], X(-1)))
    owned(0)
    t3[-1].wait_recv()
    send_t2(1, C - 1)
    for start, size in ((128, 128), (512, 256), (256, 256), (768, 256)):
        ws.append(send_w(start, size))
    s1p.append(share(HT.at[x, high], X(1)))
    s1m.append(share(HT.at[x, low], X(-1)))

    for k in range(1, C):
        owned(k)
    for n in range(4):
        turn(yl, n)

    lx = {}

    def make_layer(other, k, first, step, count):
        s = 1 - yl if other else yl

        def part(n, _):
            g, cols = (x + first + step * (n // 2)) % 4, pl.ds(pl.multiple_of((n % 2) * 256, 256), 256)
            there = pl.ds(pl.multiple_of((1 - c) * HALF + k * RL, RL), RL)
            here = pl.ds(pl.multiple_of(c * HALF + k * RL, RL), RL)
            h = HT[g, :, cols]
            LS[s, k, g, :, cols] = nn(WT[s, there, :], h).astype(BF)
            LO[s, k, g, :, cols] = nn(WT[s, here, :], h).astype(BF)
            return 0

        lax.fori_loop(0, 2 * count, part, 0)

        for n in range(count):
            g = (x + first + step * n) % 4
            lx.setdefault((other, k), []).append(cp.put(LS.at[s, k, g], LX.at[s, k, g], CORE))

    cross(0, 0)
    cross(0, 1)
    s1p[0].wait_recv()
    s1m[0].wait_recv()
    s2 = [share(HT.at[tok(-1), a0], X(1)), share(HT.at[tok(1), a1], X(-1))]
    make_layer(False, 0, 0, 1, 1)
    make_layer(False, 1, 0, 1, 1)
    s1p[1].wait_recv()
    s1m[1].wait_recv()
    s2 += [share(HT.at[tok(-1), a0b], X(1)), share(HT.at[tok(1), a1b], X(-1))]

    for k in range(C):
        for b in range(2):
            near[b, k][0].wait_recv()
            near[b, k][1].wait_recv()
            far[b, k] = forward(b, k)
        if k == 1:
            s1p[2].wait_recv()
            s1m[2].wait_recv()
            make_layer(False, 0, 1, 2, 2)
        if k == 2:
            make_layer(False, 1, 1, 2, 2)
            ws[0].wait_recv()
            ws[1].wait_recv()
            turn(1 - yl, 0)
    for b in range(2):
        cross(1, b)
        cross(-1, b)
    ws[2].wait_recv()
    turn(1 - yl, 2)
    make_layer(True, 0, 0, 1, 2)
    make_layer(True, 0, 3, 1, 1)
    for f in s2:
        f.wait_recv()
    make_layer(False, 0, 2, 1, 1)
    make_layer(True, 0, 2, 1, 1)
    for b in range(2):
        for k in range(C):
            far[b, k][0].wait_recv()
            far[b, k][1].wait_recv()
        cross(2, b)

    def weight_sum(s, n):
        cols = pl.ds(n * 256, 256)
        acc[...] = jnp.zeros_like(acc)

        def add(g, _):
            acc[...] += nt(HT[g], CT[2 * g + s, cols, :])
            return 0

        lax.fori_loop(0, 4, add, 0)

    gd = {}

    def partner_sum(n):
        weight_sum(1 - yl, n)
        GDS[n] = acc[...].astype(BF)

    def send_sum(n, start=0, size=FF):
        at = pl.ds(start, size)
        gd.setdefault(n, []).append(cp.put(GDS.at[n, at], GDR.at[n, at], YL))

    def make_grad(g):
        def part(k, _):
            cols = pl.ds(pl.multiple_of(k * 256, 256), 256)
            G[g, :, cols] = (nn(W2[0], CT[2 * g, :, cols]) + nn(W2[1], CT[2 * g + 1, :, cols])).astype(BF)
            return 0

        lax.fori_loop(0, 2, part, 0)

    def pair(dz, b, k):
        token, s = place(dz, b)
        LO[s, k, token] = (LO[s, k, token].astype(F32) + LX[s, k, token].astype(F32)).astype(BF)

    halves, directs = {}, {}

    def begin(k):
        for b in range(2):
            pair(2, b, k)
            token, s = place(2, b)
            halves[b, k] = (
                cp.put(LO.at[s, k, token, pl.ds(0, HL)], LH.at[b, 0, k], Z(1)),
                cp.put(LO.at[s, k, token, pl.ds(HL, HL)], LH.at[b, 1, k], Z(-1)),
            )
        for b in range(2):
            pair(1, b, k)
            pair(-1, b, k)

    def relay(b, k):
        sent = []
        for side, dz in ((0, 1), (1, -1)):
            token, s = place(dz, b)
            halves[b, k][side].wait_recv()
            at = pl.ds(side * HL, HL)
            LO[s, k, token, at] = (LO[s, k, token, at].astype(F32) + LH[b, side, k].astype(F32)).astype(BF)
            sent.append(cp.put(LO.at[s, k, token], LD.at[b, side, k], Z(dz)))
        directs[b, k] = sent

    PARTS = ((0, 0, RL), (1, 0, HL), (1, HL, HL))
    back_at = [cp.ids(2) for _ in PARTS]

    def send_back(b, k):
        token, s = place(0, b)
        directs[b, k][0].wait_recv()
        directs[b, k][1].wait_recv()
        LO[s, k, token] = (
            LO[s, k, token].astype(F32) + LD[b, 0, k].astype(F32) + LD[b, 1, k].astype(F32)
        ).astype(BF)
        for p, (piece, start, size) in enumerate(PARTS):
            if piece == k:
                at = pl.ds(start, size)
                sems = (back_at[p] + b, back_at[p] + x1)
                cp.put_or_keep(token == x, LO.at[s, k, token, at], BX.at[x1, k, at], owner(b), sems)

    for other in range(2):
        for f in lx[other, 0]:
            f.wait_recv()
    begin(0)
    for f in t5:
        f.wait_recv()
    partner_sum(0)
    send_sum(0)
    make_layer(False, 1, 2, 1, 1)
    ws[3].wait_recv()
    ws[4].wait_recv()
    make_grad(tok(2))
    g2a = cp.put(G.at[tok(2), low], RAB.at[low], X(1))
    g2b = cp.put(G.at[tok(2), high], RAB.at[high], X(-1))
    relay(0, 0)
    turn(1 - yl, 1)
    turn(1 - yl, 3)
    make_layer(True, 1, 0, 1, 2)
    relay(1, 0)
    make_layer(True, 1, 2, 1, 2)
    partner_sum(1)
    send_sum(1)
    for other in range(2):
        for f in lx[other, 1]:
            f.wait_recv()
    begin(1)
    for k in range(CL):
        pair(0, 0, k)
        pair(0, 1, k)
    up_one, down_one = tok(1), tok(-1)
    make_grad(up_one)
    send_back(0, 0)
    g5 = [cp.put(G.at[up_one, high], RO.at[0, high], X(1))]
    partner_sum(2)
    send_sum(2)
    send_back(1, 0)
    make_grad(down_one)
    g5.append(cp.put(G.at[down_one, low], RO.at[1, low], X(-1)))
    relay(0, 1)
    relay(1, 1)
    partner_sum(3)

    ly = []

    def meet(p):
        k, start, size = PARTS[p]
        at = pl.ds(start, size)
        for r in range(2):
            cp.landed(2 * r + hz == x, LO.at[0, 0, 0, at], BX.at[r, k, at], back_at[p] + r, owner(r))
        ly.append(cp.put(BX.at[1 - yh, k, at], BY.at[k, at], YH))

    meet(0)
    send_sum(3, 0, CUT)
    g2a.wait_recv()
    G[up_one, low] = (G[up_one, low].astype(F32) + RAB[low].astype(F32)).astype(BF)
    g2b.wait_recv()
    G[down_one, high] = (G[down_one, high].astype(F32) + RAB[high].astype(F32)).astype(BF)
    send_back(0, 1)
    send_back(1, 1)
    g5.append(cp.put(G.at[up_one, low], RO.at[0, low], X(1)))
    g5.append(cp.put(G.at[down_one, high], RO.at[1, high], X(-1)))
    make_grad(x)

    sw = []

    def home(p):
        k, start, size = PARTS[p]
        ly[p].wait_recv()
        part, at = pl.ds(start, size), pl.ds(k * RL + start, size)
        FIN[at] = (BX[yh, k, part].astype(F32) + BY[k, part].astype(F32)).astype(BF)
        sw.append(cp.put_or_keep(t1_keep, FIN.at[at], SWP.at[at], T1S)[1])

    outs = []

    def own_sum(n):
        weight_sum(yl, n)
        for f in gd[n]:
            f.wait_recv()
        if n > 1:
            outs[n - 2].wait()
        gd_stage[n % 2] = (acc[...] + GDR[n].astype(F32)).astype(BF)
        copy = pltpu.make_async_copy(gd_stage.at[n % 2], gd_out.at[:, pl.ds(n * 256, 256)], out_sem.at[n])
        copy.start()
        outs.append(copy)

    own_sum(0)
    meet(1)
    meet(2)
    send_sum(3, CUT, FF - CUT)
    home(0)
    own_sum(1)
    weight_sum(yl, 2)
    gd[2][0].wait_recv()
    outs[0].wait()
    gd_stage[0] = (acc[...] + GDR[2].astype(F32)).astype(BF)
    third = pltpu.make_async_copy(gd_stage.at[0], gd_out.at[:, pl.ds(512, 256)], out_sem.at[2])
    third.start()
    home(1)
    weight_sum(yl, 3)
    home(2)

    for f in g5:
        f.wait_recv()

    def finish(k, _):
        rows = pl.ds(pl.multiple_of(k * 32, 32), 32)
        total = G[x, rows, :].astype(F32) + RO[0, rows, :].astype(F32) + RO[1, rows, :].astype(F32)
        g = gate[rows, :].astype(F32)
        squash = jax.nn.sigmoid(g)
        gu_stage[rows, :] = (total * g * squash).astype(BF)
        gg_stage[rows, :] = (
            total * up[rows, :].astype(F32) * squash * (1.0 + g * (1.0 - squash))
        ).astype(BF)
        return 0

    lax.fori_loop(0, 29, finish, 0)
    for n, (stage, out) in enumerate(((gg_stage, gg_out), (gu_stage, gu_out))):
        copy = pltpu.make_async_copy(stage, out, out_sem.at[5 + n])
        copy.start()
        outs.append(copy)
    lays = []

    def settle(p):
        k, start, size = PARTS[p]
        at = pl.ds(k * RL + start, size)
        cp.landed(t1_keep, FIN.at[at], SWP.at[at], sw[p], T1S)
        for first in range(k * RL + start, k * RL + start + size, 128):
            n, at = first // 128, pl.ds(first, 128)
            for r in range(0, TOK, 128):
                lay_stage[n, r : r + 128, :] = SWP[at, r : r + 128].astype(F32).T.astype(BF)
            lays.append(pltpu.make_async_copy(lay_stage.at[n], lay_out.at[:, at], out_sem.at[7 + n]))
            lays[n].start()

    settle(0)
    settle(1)
    gd[3][0].wait_recv()
    gd[3][1].wait_recv()
    outs[1].wait()
    gd_stage[1] = (acc[...] + GDR[3].astype(F32)).astype(BF)
    fourth = pltpu.make_async_copy(gd_stage.at[1], gd_out.at[:, pl.ds(768, 256)], out_sem.at[3])
    fourth.start()
    cp.finish()

    settle(2)
    for copy in (outs[2], outs[3], third, fourth, *lays):
        copy.wait()


def place_outputs(*refs):
    sources, results, stages, sems = refs[:4], refs[4:8], refs[8:12], refs[12]
    arrive, leave = [], []
    for n in (0, 3, 1, 2):
        rows = sources[n].shape[0] // 2
        for part in range(2):
            at, k = pl.ds(part * rows, rows), len(arrive)
            arrive.append(pltpu.make_async_copy(sources[n].at[at], stages[n].at[at], sems.at[k]))
            leave.append(pltpu.make_async_copy(stages[n].at[at], results[n].at[at], sems.at[8 + k]))
    for copy in arrive:
        copy.start()
    for k in range(8):
        arrive[k].wait()
        leave[k].start()
    for copy in leave:
        copy.wait()


def shards(gate_pre, up_pre, w_down, cotangent):
    anywhere = pl.BlockSpec(memory_space=pl.ANY)
    n_copies = 140
    flops = 2 * 3 * TOK * FF * 8192
    shapes = (
        jax.ShapeDtypeStruct((TOK, HALF), BF),
        jax.ShapeDtypeStruct((FF, TOK), BF),
        jax.ShapeDtypeStruct((FF, TOK), BF),
        jax.ShapeDtypeStruct((FF, DM), BF),
    )
    results = pl.pallas_call(
        kernel,
        out_shape=shapes,
        in_specs=[anywhere] * 4,
        out_specs=[anywhere] * 4,
        scratch_shapes=[
            pltpu.VMEM((FF, TOK), BF),
            pltpu.VMEM((FF, TOK), BF),
            pltpu.VMEM((TOK, HALF), BF),
            pltpu.VMEM((2, FF, DM), BF),
            pltpu.VMEM((2, DM, FF), BF),
            pltpu.VMEM((4, FF, TOK), BF),
            pltpu.VMEM((8, DM, TOK), BF),
            pltpu.VMEM((HALF, TOK), BF),
            pltpu.VMEM((2, HALF, TOK), BF),
            pltpu.VMEM((4, FF, TOK), BF),
            pltpu.VMEM((FF, TOK), BF),
            pltpu.VMEM((2, FF, TOK), BF),
            pltpu.VMEM((2, CL, 4, RL, TOK), BF),
            pltpu.VMEM((2, CL, 4, RL, TOK), BF),
            pltpu.VMEM((2, CL, 4, RL, TOK), BF),
            pltpu.VMEM((2, 2, CL, HL, TOK), BF),
            pltpu.VMEM((2, 2, CL, RL, TOK), BF),
            pltpu.VMEM((2, CL, RL, TOK), BF),
            pltpu.VMEM((CL, RL, TOK), BF),
            pltpu.VMEM((HALF, TOK), BF),
            pltpu.VMEM((HALF, TOK), BF),
            pltpu.VMEM((FF, 256), F32),
            pltpu.VMEM((4, FF, 256), BF),
            pltpu.VMEM((4, FF, 256), BF),
            pltpu.VMEM((2, FF, 256), BF),
            pltpu.VMEM((HALF // 128, TOK, 128), BF),
            pltpu.VMEM((FF, TOK), BF),
            pltpu.VMEM((FF, TOK), BF),
            pltpu.SemaphoreType.DMA((n_copies,)),
            pltpu.SemaphoreType.DMA((n_copies,)),
            pltpu.SemaphoreType.DMA((4,)),
            pltpu.SemaphoreType.DMA((7 + HALF // 128,)),
        ],
        compiler_params=pltpu.CompilerParams(
            collective_id=0, has_side_effects=True, vmem_limit_bytes=64 * 2**20
        ),
        cost_estimate=pl.CostEstimate(flops=flops, bytes_accessed=2**24, transcendentals=0),
    )(gate_pre.T, up_pre.T, w_down, cotangent)
    layer_out, grad_gate, grad_up, grad_down = pl.pallas_call(
        place_outputs,
        out_shape=shapes,
        in_specs=[anywhere] * 4,
        out_specs=[anywhere] * 4,
        scratch_shapes=[pltpu.VMEM(shape.shape, BF) for shape in shapes] + [pltpu.SemaphoreType.DMA((16,))],
        compiler_params=pltpu.CompilerParams(vmem_limit_bytes=64 * 2**20),
    )(*results)
    return layer_out, grad_gate.T, grad_up.T, grad_down


def solution(mesh):
    placed = (P("dp", "tensor"), P("dp", "tensor"), P("tensor", "dp"), P("dp", "tensor"))
    return jax.shard_map(
        shards,
        mesh=mesh,
        in_specs=placed,
        out_specs=(P("dp", "tensor"), P("dp", "tensor"), P("dp", "tensor"), P("tensor", "dp")),
        check_vma=False,
    )
```

```python
import jax
import jax.numpy as jnp
from jax import lax
from jax.experimental import pallas as pl
from jax.experimental.pallas import tpu as pltpu
from jax.sharding import PartitionSpec as P

MESH = pl.DeviceIdType.MESH
BF = jnp.bfloat16
F32 = jnp.float32

TOK = 512
FF = 928
DM = 1024
HALF = 512
CUT = 464
C = 4
RC = HALF // C
HC = RC // 2
CL = 2
RL = HALF // CL
HL = RL // 2


class Copies:
    def __init__(self, send, recv):
        self.send, self.recv, self.all, self.n = send, recv, [], 0

    def ids(self, count):
        self.n += count
        return self.n - count

    def put(self, src, dst, target):
        k = self.ids(1)
        copy = pltpu.make_async_remote_copy(
            src, dst, self.send.at[k], self.recv.at[k], device_id=target, device_id_type=MESH
        )
        copy.start()
        self.all.append((None, copy))
        return copy

    def put_or_keep(self, keep, src, dst, target, at=None):
        ks, kr = at or (self.ids(1),) * 2
        copy = pltpu.make_async_remote_copy(
            src, dst, self.send.at[ks], self.recv.at[kr], device_id=target, device_id_type=MESH
        )
        pl.when(keep)(pltpu.make_async_copy(src, dst, self.recv.at[kr]).start)
        pl.when(jnp.logical_not(keep))(copy.start)
        self.all.append((keep, copy))
        return ks, kr

    def landed(self, keep, src, landing, kr, target):
        got = pltpu.make_async_remote_copy(
            src, landing, self.send.at[kr], self.recv.at[kr], device_id=target, device_id_type=MESH
        )
        pl.when(keep)(pltpu.make_async_copy(src, landing, self.recv.at[kr]).wait)
        pl.when(jnp.logical_not(keep))(got.wait_recv)

    def finish(self):
        for keep, copy in self.all:
            if keep is None:
                copy.wait_send()
            else:
                pl.when(jnp.logical_not(keep))(copy.wait_send)
        self.all = []


def nn(a, b):
    return lax.dot_general(a, b, (((1,), (0,)), ((), ())), preferred_element_type=F32)


def nt(a, b):
    return lax.dot_general(a, b, (((1,), (1,)), ((), ())), preferred_element_type=F32)


def kernel(
    gate_in, up_in, w_in, cot_in, lay_out, gg_out, gu_out, gd_out,
    gate, up, cot, W2, WT, HT, CT, OWN, ZM, G, RAB, RO, LO, LS, LX, LH, LD, BX, BY, FIN, SWP,
    acc, GDS, GDR, gd_stage, lay_stage, gg_stage, gu_stage, send_sem, recv_sem, in_sem, out_sem,
):
    dp, t = lax.axis_index("dp"), lax.axis_index("tensor")
    x, yl = dp // 2, dp % 2
    yh, z, c = t // 8, (t // 2) % 4, t % 2
    x1, x0, z1, z0 = x // 2, x % 2, z // 2, z % 2

    def X(d):
        return (((x + d + 4) % 4) * 2 + yl, t)

    def Z(d):
        return (dp, yh * 8 + ((z + d + 4) % 4) * 2 + c)

    YL = (x * 2 + 1 - yl, t)
    YH = (dp, (1 - yh) * 8 + z * 2 + c)
    CORE = (dp, t + 1 - 2 * c)
    T1 = (dp, yh * 8 + (2 * z0 + (x0 + z1) % 2) * 2 + c)
    T1S = (dp, yh * 8 + (2 * ((x0 + z0) % 2) + z1) * 2 + c)
    hz = (x0 + z0) % 2
    t1_keep = T1[1] == t

    def owner(b):
        return ((2 * b + hz) * 2 + yl, t)

    def tok(dx):
        return (x + dx + 4) % 4

    def place(dz, b):
        at = (z + dz + 4) % 4
        return 2 * b + (x0 + at) % 2, at // 2

    barrier = pltpu.get_barrier_semaphore()
    greeted = (X(1), X(-1), YL, Z(1), Z(-1), YH, CORE, T1, T1S, owner(0), owner(1))
    for other in greeted:
        pl.semaphore_signal(barrier, inc=1, device_id=other, device_id_type=MESH)
    loads = []
    for n, (src, dst) in enumerate(((cot_in, cot), (gate_in, gate), (up_in, up), (w_in, W2.at[yl]))):
        loads.append(pltpu.make_async_copy(src, dst, in_sem.at[n]))
        loads[-1].start()

    def make_hidden(k, _):
        rows = pl.ds(pl.multiple_of(k * 32, 32), 32)
        g = gate[rows, :].astype(F32)
        HT[x, rows, :] = (g * jax.nn.sigmoid(g) * up[rows, :].astype(F32)).astype(BF)
        return 0

    loads[0].wait()
    for r in range(0, HALF, 128):
        OWN[:, r : r + 128] = cot[r : r + 128, :].astype(F32).T.astype(BF)

    pl.semaphore_wait(barrier, len(greeted))
    cp = Copies(send_sem, recv_sem)
    low, high = pl.ds(0, CUT), pl.ds(CUT, FF - CUT)

    def crow(k, size=RC):
        return pl.ds(pl.multiple_of(c * HALF + k, 16), size)

    def share(ref, target):
        return cp.put(ref, ref, target)

    t1 = []
    for k in range(C):
        at = pl.ds(k * RC, RC)
        t1.append(cp.put_or_keep(t1_keep, OWN.at[at], ZM.at[0, at], T1)[1])

    loads[1].wait()
    loads[2].wait()
    lax.fori_loop(0, 29, make_hidden, 0)
    a0, a1 = pl.ds(0, 240), pl.ds(FF - 240, 240)
    a0b, a1b = pl.ds(240, CUT - 240), pl.ds(CUT, FF - 240 - CUT)
    s1p, s1m = [share(HT.at[x, a0], X(1))], [share(HT.at[x, a1], X(-1))]
    loads[3].wait()

    def send_w(start, size):
        return share(W2.at[yl, :, pl.ds(start, size)], YL)

    ws = [send_w(0, 128)]

    def turn(s, n):
        WT[s, pl.ds(n * 256, 256), :] = W2[s, :, pl.ds(n * 256, 256)].astype(F32).T.astype(BF)

    t2_at = [cp.ids(2) for _ in range(C)]

    def send_t2(n, k):
        b = (n + yh) % 2
        at = pl.ds(k * RC, RC)
        cp.put_or_keep(
            2 * b + hz == x, ZM.at[n, at], CT.at[2 * x + z1, crow(k * RC)], owner(b), (t2_at[k] + n, t2_at[k] + x1)
        )

    def spread(b, k):
        token, s = place(0, b)
        ref = CT.at[2 * token + s, crow(k * RC)]
        return share(ref, Z(1)), share(ref, Z(-1))

    def forward(b, k):
        token, s = place(-1, b)
        lower = CT.at[2 * token + s, crow(k * RC, HC)]
        token, s = place(1, b)
        upper = CT.at[2 * token + s, crow(k * RC + HC, HC)]
        return share(lower, Z(1)), share(upper, Z(-1))

    t5, near, far = [], {}, {}

    def cross(dz, b):
        token, s = place(dz, b)
        t5.append(share(CT.at[2 * token + s, crow(0, HALF)], CORE))

    def owned(k):
        for b in range(2):
            landing = CT.at[2 * (2 * b + hz) + z1, crow(k * RC)]
            cp.landed(2 * b + hz == x, ZM.at[0, pl.ds(k * RC, RC)], landing, t2_at[k] + b, owner(b))
            near[b, k] = spread(b, k)

    t3 = []
    for k in range(C):
        at = pl.ds(k * RC, RC)
        cp.landed(t1_keep, OWN.at[at], ZM.at[0, at], t1[k], T1)
        t3.append(cp.put(ZM.at[0, at], ZM.at[1, at], YH))
        send_t2(0, k)
        if k > 0:
            t3[k - 1].wait_recv()
            send_t2(1, k - 1)
        if k == 1:
            s1p.append(share(HT.at[x, a0b], X(1)))
            s1m.append(share(HT.at[x, a1b], X(-1)))
    owned(0)
    t3[-1].wait_recv()
    send_t2(1, C - 1)
    for start, size in ((128, 128), (512, 256), (256, 256), (768, 256)):
        ws.append(send_w(start, size))
    s1p.append(share(HT.at[x, high], X(1)))
    s1m.append(share(HT.at[x, low], X(-1)))

    for k in range(1, C):
        owned(k)
    for n in range(4):
        turn(yl, n)

    lx = {}

    def make_layer(other, k, first, step, count):
        s = 1 - yl if other else yl

        def part(n, _):
            g, cols = (x + first + step * (n // 2)) % 4, pl.ds(pl.multiple_of((n % 2) * 256, 256), 256)
            there = pl.ds(pl.multiple_of((1 - c) * HALF + k * RL, RL), RL)
            here = pl.ds(pl.multiple_of(c * HALF + k * RL, RL), RL)
            h = HT[g, :, cols]
            LS[s, k, g, :, cols] = nn(WT[s, there, :], h).astype(BF)
            LO[s, k, g, :, cols] = nn(WT[s, here, :], h).astype(BF)
            return 0

        lax.fori_loop(0, 2 * count, part, 0)

        for n in range(count):
            g = (x + first + step * n) % 4
            lx.setdefault((other, k), []).append(cp.put(LS.at[s, k, g], LX.at[s, k, g], CORE))

    cross(0, 0)
    cross(0, 1)
    s1p[0].wait_recv()
    s1m[0].wait_recv()
    s2 = [share(HT.at[tok(-1), a0], X(1)), share(HT.at[tok(1), a1], X(-1))]
    make_layer(False, 0, 0, 1, 1)
    make_layer(False, 1, 0, 1, 1)
    s1p[1].wait_recv()
    s1m[1].wait_recv()
    s2 += [share(HT.at[tok(-1), a0b], X(1)), share(HT.at[tok(1), a1b], X(-1))]

    for k in range(C):
        for b in range(2):
            near[b, k][0].wait_recv()
            near[b, k][1].wait_recv()
            far[b, k] = forward(b, k)
        if k == 1:
            s1p[2].wait_recv()
            s1m[2].wait_recv()
            make_layer(False, 0, 1, 2, 2)
        if k == 2:
            make_layer(False, 1, 1, 2, 2)
            ws[0].wait_recv()
            ws[1].wait_recv()
            turn(1 - yl, 0)
    for b in range(2):
        cross(1, b)
        cross(-1, b)
    ws[2].wait_recv()
    turn(1 - yl, 2)
    make_layer(True, 0, 0, 1, 2)
    make_layer(True, 0, 3, 1, 1)
    for f in s2:
        f.wait_recv()
    make_layer(False, 0, 2, 1, 1)
    make_layer(True, 0, 2, 1, 1)
    for b in range(2):
        for k in range(C):
            far[b, k][0].wait_recv()
            far[b, k][1].wait_recv()
        cross(2, b)

    def weight_sum(s, n):
        cols = pl.ds(n * 256, 256)
        acc[...] = jnp.zeros_like(acc)

        def add(g, _):
            acc[...] += nt(HT[g], CT[2 * g + s, cols, :])
            return 0

        lax.fori_loop(0, 4, add, 0)

    gd = {}

    def partner_sum(n):
        weight_sum(1 - yl, n)
        GDS[n] = acc[...].astype(BF)

    def send_sum(n, start=0, size=FF):
        at = pl.ds(start, size)
        gd.setdefault(n, []).append(cp.put(GDS.at[n, at], GDR.at[n, at], YL))

    def make_grad(g):
        def part(k, _):
            cols = pl.ds(pl.multiple_of(k * 256, 256), 256)
            G[g, :, cols] = (nn(W2[0], CT[2 * g, :, cols]) + nn(W2[1], CT[2 * g + 1, :, cols])).astype(BF)
            return 0

        lax.fori_loop(0, 2, part, 0)

    def pair(dz, b, k):
        token, s = place(dz, b)
        LO[s, k, token] = (LO[s, k, token].astype(F32) + LX[s, k, token].astype(F32)).astype(BF)

    halves, directs = {}, {}

    def begin(k):
        for b in range(2):
            pair(2, b, k)
            token, s = place(2, b)
            halves[b, k] = (
                cp.put(LO.at[s, k, token, pl.ds(0, HL)], LH.at[b, 0, k], Z(1)),
                cp.put(LO.at[s, k, token, pl.ds(HL, HL)], LH.at[b, 1, k], Z(-1)),
            )
        for b in range(2):
            pair(1, b, k)
            pair(-1, b, k)

    def relay(b, k):
        sent = []
        for side, dz in ((0, 1), (1, -1)):
            token, s = place(dz, b)
            halves[b, k][side].wait_recv()
            at = pl.ds(side * HL, HL)
            LO[s, k, token, at] = (LO[s, k, token, at].astype(F32) + LH[b, side, k].astype(F32)).astype(BF)
            sent.append(cp.put(LO.at[s, k, token], LD.at[b, side, k], Z(dz)))
        directs[b, k] = sent

    PARTS = ((0, 0, RL), (1, 0, HL), (1, HL, HL))
    back_at = [cp.ids(2) for _ in PARTS]

    def send_back(b, k):
        token, s = place(0, b)
        directs[b, k][0].wait_recv()
        directs[b, k][1].wait_recv()
        LO[s, k, token] = (
            LO[s, k, token].astype(F32) + LD[b, 0, k].astype(F32) + LD[b, 1, k].astype(F32)
        ).astype(BF)
        for p, (piece, start, size) in enumerate(PARTS):
            if piece == k:
                at = pl.ds(start, size)
                sems = (back_at[p] + b, back_at[p] + x1)
                cp.put_or_keep(token == x, LO.at[s, k, token, at], BX.at[x1, k, at], owner(b), sems)

    for other in range(2):
        for f in lx[other, 0]:
            f.wait_recv()
    begin(0)
    for f in t5:
        f.wait_recv()
    partner_sum(0)
    send_sum(0)
    make_layer(False, 1, 2, 1, 1)
    ws[3].wait_recv()
    ws[4].wait_recv()
    make_grad(tok(2))
    g2a = cp.put(G.at[tok(2), low], RAB.at[low], X(1))
    g2b = cp.put(G.at[tok(2), high], RAB.at[high], X(-1))
    relay(0, 0)
    turn(1 - yl, 1)
    turn(1 - yl, 3)
    make_layer(True, 1, 0, 1, 2)
    relay(1, 0)
    make_layer(True, 1, 2, 1, 2)
    partner_sum(1)
    send_sum(1)
    for other in range(2):
        for f in lx[other, 1]:
            f.wait_recv()
    begin(1)
    for k in range(CL):
        pair(0, 0, k)
        pair(0, 1, k)
    up_one, down_one = tok(1), tok(-1)
    make_grad(up_one)
    send_back(0, 0)
    g5 = [cp.put(G.at[up_one, high], RO.at[0, high], X(1))]
    partner_sum(2)
    send_sum(2)
    send_back(1, 0)
    make_grad(down_one)
    g5.append(cp.put(G.at[down_one, low], RO.at[1, low], X(-1)))
    relay(0, 1)
    relay(1, 1)
    partner_sum(3)

    ly = []

    def meet(p):
        k, start, size = PARTS[p]
        at = pl.ds(start, size)
        for r in range(2):
            cp.landed(2 * r + hz == x, LO.at[0, 0, 0, at], BX.at[r, k, at], back_at[p] + r, owner(r))
        ly.append(cp.put(BX.at[1 - yh, k, at], BY.at[k, at], YH))

    meet(0)
    send_sum(3, 0, CUT)
    g2a.wait_recv()
    G[up_one, low] = (G[up_one, low].astype(F32) + RAB[low].astype(F32)).astype(BF)
    g2b.wait_recv()
    G[down_one, high] = (G[down_one, high].astype(F32) + RAB[high].astype(F32)).astype(BF)
    send_back(0, 1)
    send_back(1, 1)
    g5.append(cp.put(G.at[up_one, low], RO.at[0, low], X(1)))
    g5.append(cp.put(G.at[down_one, high], RO.at[1, high], X(-1)))
    make_grad(x)

    sw = []

    def home(p):
        k, start, size = PARTS[p]
        ly[p].wait_recv()
        part, at = pl.ds(start, size), pl.ds(k * RL + start, size)
        FIN[at] = (BX[yh, k, part].astype(F32) + BY[k, part].astype(F32)).astype(BF)
        sw.append(cp.put_or_keep(t1_keep, FIN.at[at], SWP.at[at], T1S)[1])

    outs = []

    def own_sum(n):
        weight_sum(yl, n)
        for f in gd[n]:
            f.wait_recv()
        if n > 1:
            outs[n - 2].wait()
        gd_stage[n % 2] = (acc[...] + GDR[n].astype(F32)).astype(BF)
        copy = pltpu.make_async_copy(gd_stage.at[n % 2], gd_out.at[:, pl.ds(n * 256, 256)], out_sem.at[n])
        copy.start()
        outs.append(copy)

    lays = []

    def settle(p):
        k, start, size = PARTS[p]
        at = pl.ds(k * RL + start, size)
        cp.landed(t1_keep, FIN.at[at], SWP.at[at], sw[p], T1S)
        for first in range(k * RL + start, k * RL + start + size, 128):
            n, at = first // 128, pl.ds(first, 128)
            for r in range(0, TOK, 128):
                lay_stage[n, r : r + 128, :] = SWP[at, r : r + 128].astype(F32).T.astype(BF)
            lays.append(pltpu.make_async_copy(lay_stage.at[n], lay_out.at[:, at], out_sem.at[7 + n]))
            lays[n].start()

    own_sum(0)
    meet(1)
    meet(2)
    send_sum(3, CUT, FF - CUT)
    home(0)
    own_sum(1)
    weight_sum(yl, 2)
    gd[2][0].wait_recv()
    outs[0].wait()
    gd_stage[0] = (acc[...] + GDR[2].astype(F32)).astype(BF)
    third = pltpu.make_async_copy(gd_stage.at[0], gd_out.at[:, pl.ds(512, 256)], out_sem.at[2])
    third.start()
    home(1)
    weight_sum(yl, 3)
    settle(0)
    home(2)

    for f in g5:
        f.wait_recv()

    def finish(k, _):
        rows = pl.ds(pl.multiple_of(k * 32, 32), 32)
        total = G[x, rows, :].astype(F32) + RO[0, rows, :].astype(F32) + RO[1, rows, :].astype(F32)
        g = gate[rows, :].astype(F32)
        squash = jax.nn.sigmoid(g)
        gu_stage[rows, :] = (total * g * squash).astype(BF)
        gg_stage[rows, :] = (
            total * up[rows, :].astype(F32) * squash * (1.0 + g * (1.0 - squash))
        ).astype(BF)
        return 0

    lax.fori_loop(0, 29, finish, 0)
    for n, (stage, out) in enumerate(((gg_stage, gg_out), (gu_stage, gu_out))):
        copy = pltpu.make_async_copy(stage, out, out_sem.at[5 + n])
        copy.start()
        outs.append(copy)
    settle(1)
    gd[3][0].wait_recv()
    gd[3][1].wait_recv()
    outs[1].wait()
    gd_stage[1] = (acc[...] + GDR[3].astype(F32)).astype(BF)
    fourth = pltpu.make_async_copy(gd_stage.at[1], gd_out.at[:, pl.ds(768, 256)], out_sem.at[3])
    fourth.start()
    cp.finish()

    settle(2)
    for copy in (outs[2], outs[3], third, fourth, *lays):
        copy.wait()


def place_outputs(*refs):
    sources, results, stages, sems = refs[:4], refs[4:8], refs[8:12], refs[12]
    arrive, leave = [], []
    for n in (0, 3, 1, 2):
        rows = sources[n].shape[0]
        for part in range(4):
            start = part * rows // 64 * 16
            at, k = pl.ds(start, (part + 1) * rows // 64 * 16 - start), len(arrive)
            arrive.append(pltpu.make_async_copy(sources[n].at[at], stages[n].at[at], sems.at[k]))
            leave.append(pltpu.make_async_copy(stages[n].at[at], results[n].at[at], sems.at[16 + k]))
    for copy in arrive:
        copy.start()
    for k in range(16):
        arrive[k].wait()
        leave[k].start()
    for copy in leave:
        copy.wait()


def shards(gate_pre, up_pre, w_down, cotangent):
    anywhere = pl.BlockSpec(memory_space=pl.ANY)
    n_copies = 140
    flops = 2 * 3 * TOK * FF * 8192
    shapes = (
        jax.ShapeDtypeStruct((TOK, HALF), BF),
        jax.ShapeDtypeStruct((FF, TOK), BF),
        jax.ShapeDtypeStruct((FF, TOK), BF),
        jax.ShapeDtypeStruct((FF, DM), BF),
    )
    results = pl.pallas_call(
        kernel,
        out_shape=shapes,
        in_specs=[anywhere] * 4,
        out_specs=[anywhere] * 4,
        scratch_shapes=[
            pltpu.VMEM((FF, TOK), BF),
            pltpu.VMEM((FF, TOK), BF),
            pltpu.VMEM((TOK, HALF), BF),
            pltpu.VMEM((2, FF, DM), BF),
            pltpu.VMEM((2, DM, FF), BF),
            pltpu.VMEM((4, FF, TOK), BF),
            pltpu.VMEM((8, DM, TOK), BF),
            pltpu.VMEM((HALF, TOK), BF),
            pltpu.VMEM((2, HALF, TOK), BF),
            pltpu.VMEM((4, FF, TOK), BF),
            pltpu.VMEM((FF, TOK), BF),
            pltpu.VMEM((2, FF, TOK), BF),
            pltpu.VMEM((2, CL, 4, RL, TOK), BF),
            pltpu.VMEM((2, CL, 4, RL, TOK), BF),
            pltpu.VMEM((2, CL, 4, RL, TOK), BF),
            pltpu.VMEM((2, 2, CL, HL, TOK), BF),
            pltpu.VMEM((2, 2, CL, RL, TOK), BF),
            pltpu.VMEM((2, CL, RL, TOK), BF),
            pltpu.VMEM((CL, RL, TOK), BF),
            pltpu.VMEM((HALF, TOK), BF),
            pltpu.VMEM((HALF, TOK), BF),
            pltpu.VMEM((FF, 256), F32),
            pltpu.VMEM((4, FF, 256), BF),
            pltpu.VMEM((4, FF, 256), BF),
            pltpu.VMEM((2, FF, 256), BF),
            pltpu.VMEM((HALF // 128, TOK, 128), BF),
            pltpu.VMEM((FF, TOK), BF),
            pltpu.VMEM((FF, TOK), BF),
            pltpu.SemaphoreType.DMA((n_copies,)),
            pltpu.SemaphoreType.DMA((n_copies,)),
            pltpu.SemaphoreType.DMA((4,)),
            pltpu.SemaphoreType.DMA((7 + HALF // 128,)),
        ],
        compiler_params=pltpu.CompilerParams(
            collective_id=0, has_side_effects=True, vmem_limit_bytes=64 * 2**20
        ),
        cost_estimate=pl.CostEstimate(flops=flops, bytes_accessed=2**24, transcendentals=0),
    )(gate_pre.T, up_pre.T, w_down, cotangent)
    layer_out, grad_gate, grad_up, grad_down = pl.pallas_call(
        place_outputs,
        out_shape=shapes,
        in_specs=[anywhere] * 4,
        out_specs=[anywhere] * 4,
        scratch_shapes=[pltpu.VMEM(shape.shape, BF) for shape in shapes] + [pltpu.SemaphoreType.DMA((32,))],
        compiler_params=pltpu.CompilerParams(vmem_limit_bytes=64 * 2**20),
    )(*results)
    return layer_out, grad_gate.T, grad_up.T, grad_down


def solution(mesh):
    placed = (P("dp", "tensor"), P("dp", "tensor"), P("tensor", "dp"), P("dp", "tensor"))
    return jax.shard_map(
        shards,
        mesh=mesh,
        in_specs=placed,
        out_specs=(P("dp", "tensor"), P("dp", "tensor"), P("dp", "tensor"), P("tensor", "dp")),
        check_vma=False,
    )
```
